256 devices in a mesh: dp: 32 (over y, z), tensor: 8 (over x, core).
Axes of the slice: x: 4, y: 4, z: 8, core: 2. Of those that a mesh axis runs over, the one named last changes fastest.
Arguments:
- acts: bfloat16 [32768, 5120], P('dp', 'tensor'), may hold values from -6 to 6
- out_grad: bfloat16 [32768, 2048], P(('dp', 'tensor')), may hold values from -0.1875 to 0.1875
- momentum: float32 [163840, 2048], P(('dp', 'tensor')), may hold values from -100 to 100
- q_basis: float32 [2048, 256], P('tensor'), may hold values from -0.125 to 0.125
Outputs:
- new_momentum: float32 [163840, 2048], P(('dp', 'tensor'))
- ortho: float32 [5120, 256], P('tensor')
- new_q: float32 [2048, 256], P('tensor')
The draws below stay inside these ranges and needn't reach their ends.
All inputs are finite; a program needn't handle non-finite values.
Results may differ from the reference program's by a relative error of at most 0.0003.
Values may be sent and summed in bfloat16 or wider, within the bound.
A program may use at most 64 MiB of HBM per device.

```python
import math
import jax
import jax.numpy as jnp
from jax import lax

D_IN = 5120
D_OUT = 2048
RANK = 256
TOK = 1024
TOKENS = 32768
N_DP = 32


def draw_momentum(key, part):
    key_base, key_rows, key_cols = jax.random.split(key, 3)
    base = jnp.clip(jax.random.normal(key_base, (N_DP * D_IN, D_OUT), jnp.float32), -6.0, 6.0)
    row_scale = jnp.exp(jax.random.uniform(key_rows, (N_DP * D_IN, 1), jnp.float32, math.log(0.5), math.log(2.0)))
    col_scale = jnp.exp(jax.random.uniform(key_cols, (1, D_OUT), jnp.float32, math.log(0.3), math.log(3.0)))
    return jnp.clip(base * row_scale * col_scale, -100.0, 100.0)


def block_scale(stream_key, dims, shards, low, largest):
    def one(dim, shards_of):
        draws = jax.random.uniform(jax.random.fold_in(jax.random.fold_in(stream_key, 6), dim), (shards_of,), jnp.float32, low / len(shards), largest / len(shards))
        return jnp.repeat(jnp.exp(draws), dims[dim] // shards_of).reshape((-1,) + (1,) * (len(dims) - dim - 1))

    factor_of = one(*shards[0])
    for cut in shards[1:]:
        factor_of = factor_of * one(*cut)
    return factor_of


def gaussian(rng, dims, scale, reach, cuts=(), held_as=jnp.bfloat16):
    level = block_scale(rng, dims, cuts, -0.22, 0.18) if cuts else 1.0
    drawn = jax.random.normal(rng, dims, jnp.float32) * scale * level
    return jnp.minimum(jnp.maximum(drawn, -reach), reach).astype(held_as)


def setup_inputs(seed: int = 0) -> dict:
    keys = jax.random.split(jax.random.key(seed), 5)
    return {
        "acts": gaussian(keys[0], (TOKENS, D_IN), 1.0, 6.0, ((0, 32), (1, 8))),
        "out_grad": gaussian(keys[1], (TOKENS, D_OUT), TOK ** -0.5, 0.1875, ((0, 256),)),
        "momentum": draw_momentum(jax.random.fold_in(keys[4], 71), 0),
        "q_basis": gaussian(keys[3], (D_OUT, RANK), D_OUT ** -0.5, 0.125, ((0, 8),), jnp.float32),
    }


def reference(acts, out_grad, momentum, q_basis):
    rows = acts.reshape(N_DP, TOK, D_IN)
    grads_out = out_grad.reshape(N_DP, TOK, D_OUT)
    moments = momentum.reshape(N_DP, D_IN, D_OUT)

    def make_buffer(index):
        grad = lax.dot_general(rows[index].astype(jnp.float32), grads_out[index].astype(jnp.float32), (((0,), (0,)), ((), ())), preferred_element_type=jnp.float32)
        return 0.95 * moments[index] + grad
    buffers = lax.map(make_buffer, jnp.arange(N_DP, dtype=jnp.int32))
    left = jnp.einsum('nij,jr->ir', buffers, q_basis, precision=lax.Precision.HIGHEST) / N_DP
    gram = jnp.dot(left.T, left, precision=lax.Precision.HIGHEST)
    chol = jnp.linalg.cholesky(gram)
    ortho = lax.linalg.triangular_solve(chol, left, left_side=False, lower=True, transpose_a=True)
    right = jnp.einsum('nij,ir->jr', buffers, ortho, precision=lax.Precision.HIGHEST) / N_DP
    update = jnp.dot(ortho, right.T, precision=lax.Precision.HIGHEST)
    new_momentum = (buffers - 0.05 * update[None]).reshape(N_DP * D_IN, D_OUT)
    new_q = right * lax.rsqrt(lax.optimization_barrier(jnp.sum(right * right, axis=0, keepdims=True)) + 1e-06)
    return (new_momentum, ortho, new_q)
```

```python
import jax
import jax.numpy as jnp
from jax import lax
from jax.experimental import pallas as pl
from jax.experimental.pallas import tpu as pltpu
from jax.sharding import Mesh
from jax.sharding import PartitionSpec as P

DP = ("dp_0", "dp_1")
TENSOR = ("tensor_0", "tensor_1")
DP_TENSOR = ("dp_0", "dp_1", "tensor_0", "tensor_1")
HIGH = lax.Precision.HIGHEST
F32, BF16 = jnp.float32, jnp.bfloat16
MESH = pl.DeviceIdType.MESH


def halves(value):
    high = value.astype(BF16)
    return high, (value - high.astype(F32)).astype(BF16)


def mxu(a, b):
    return lax.dot_general(a, b, (((1,), (0,)), ((), ())), preferred_element_type=F32)


class Place:
    def __init__(self):
        self.y, self.z = lax.axis_index("dp_0"), lax.axis_index("dp_1")
        self.x, self.c = lax.axis_index("tensor_0"), lax.axis_index("tensor_1")
        step = 1 - 2 * self.c
        self.sib = 1 - self.c
        self.xp, self.xm = lax.rem(self.x + step + 4, 4), lax.rem(self.x - step + 4, 4)
        self.yp, self.ym = lax.rem(self.y + step + 4, 4), lax.rem(self.y - step + 4, 4)
        self.xo, self.yo = lax.rem(self.x + 2, 4), lax.rem(self.y + 2, 4)

    def zk(self, k):
        return lax.rem(self.z + k, 8)


def greet(me):
    barrier = pltpu.get_barrier_semaphore()
    targets = [{"tensor_1": me.sib}, {"tensor_0": me.xp}, {"tensor_0": me.xm}]
    targets += [{"dp_0": me.yp}, {"dp_0": me.ym}]
    targets += [{"dp_1": me.zk(k)} for k in range(1, 8)]
    for target in targets:
        pl.semaphore_signal(barrier, inc=1, device_id=target, device_id_type=MESH)
    pl.semaphore_wait(barrier, len(targets))


class Links:
    def __init__(self, send, recv):
        self.send, self.recv, self.used, self.sent = send, recv, 0, []

    def to(self, src, dst, target):
        copy = pltpu.make_async_remote_copy(
            src_ref=src,
            dst_ref=dst,
            send_sem=self.send.at[self.used],
            recv_sem=self.recv.at[self.used],
            device_id=target,
            device_id_type=MESH,
        )
        self.used += 1
        copy.start()
        self.sent.append(copy)
        return copy

    def finish(self):
        for copy in self.sent:
            copy.wait_send()


class Gather:
    def __init__(self, me, links, own, slot):
        self.me, self.links, self.slot = me, links, slot
        here = slot(me.x, me.c)
        self.a = links.to(own, here, {"tensor_0": me.xp})
        self.b = links.to(own, here, {"tensor_0": me.xm})
        self.s0 = links.to(own, here, {"tensor_1": me.sib})

    def first(self):
        me = self.me
        self.a.wait_recv()
        block = self.slot(me.xm, me.c)
        self.f = self.links.to(block, block, {"tensor_0": me.xp})
        self.s1 = self.links.to(block, block, {"tensor_1": me.sib})

    def second(self):
        me = self.me
        self.b.wait_recv()
        block = self.slot(me.xp, me.c)
        self.s2 = self.links.to(block, block, {"tensor_1": me.sib})

    def third(self):
        me = self.me
        self.f.wait_recv()
        block = self.slot(me.xo, me.c)
        self.s3 = self.links.to(block, block, {"tensor_1": me.sib})

    def rest(self):
        for copy in (self.s0, self.s1, self.s2, self.s3):
            copy.wait_recv()


def left_kernel(
    acts, og, mom, q, buf_out, left_out,
    actsv, acts_t, buf, qg, qh, ql, yg, yh, yl, ogg,
    part, r0, r1, r2, s1, chunk, zr, zs, full, send, recv, local,
):
    me = Place()
    links = Links(send, recv)
    own_q = qg.at[me.x * 2 + me.c]
    own_rows = pl.ds(pl.multiple_of(me.c * 128, 128), 128)
    own_og = ogg.at[me.x, own_rows]
    loads = [
        pltpu.make_async_copy(q, own_q, local.at[0]),
        pltpu.make_async_copy(og, own_og, local.at[1]),
        pltpu.make_async_copy(acts, actsv, local.at[2]),
        pltpu.make_async_copy(mom, buf, local.at[3]),
    ]
    for load in loads:
        load.start()
    greet(me)
    gq = Gather(me, links, q, lambda x, c: qg.at[x * 2 + c])
    loads[2].wait()
    for j in range(4):
        acts_t[j] = actsv[256 * j : 256 * (j + 1), :].T
    gq.first()
    gq.second()
    gq.third()
    loads[0].wait()
    gq.rest()

    @pl.loop(0, 8)
    def _(b):
        high, low = halves(qg[b])
        rows = pl.ds(pl.multiple_of(b * 256, 256), 256)
        qh[rows], ql[rows] = high, low

    loads[1].wait()
    own = ogg[me.x, own_rows, :]
    own_y = yg.at[me.x, own_rows]
    yg[me.x, own_rows, :] = mxu(own, qh[...]) + mxu(own, ql[...])
    gy = Gather(me, links, own_y, lambda x, c: yg.at[x, pl.ds(pl.multiple_of(c * 128, 128), 128)])
    loads[3].wait()

    def momentum_part(t):
        rows = pl.ds(pl.multiple_of(t * 128, 128), 128)
        high, low = halves(buf[rows, :])
        acc = mxu(high, qh[...]) + mxu(high, ql[...]) + mxu(low, qh[...])
        acc = acc * (0.95 / 32)
        part[0, rows, :] = acc[:, :128]
        part[1, rows, :] = acc[:, 128:]

    pl.loop(0, 2)(momentum_part)
    gy.first()
    gy.second()
    pl.loop(2, 5)(momentum_part)
    gy.third()
    gy.rest()
    go = Gather(
        me, links, og, lambda x, c: ogg.at[x, pl.ds(pl.multiple_of(c * 128, 128), 128)]
    )
    for j in range(4):
        high, low = halves(yg[j])
        yh[j], yl[j] = high, low

    @pl.loop(0, 5)
    def _(t):
        rows = pl.ds(pl.multiple_of(t * 128, 128), 128)
        acc = jnp.zeros((128, 256), F32)
        for j in range(4):
            lhs = acts_t[j, rows, :]
            acc += mxu(lhs, yh[j]) + mxu(lhs, yl[j])
        acc = acc * (1 / 32)
        part[0, rows, :] += acc[:, :128]
        part[1, rows, :] += acc[:, 128:]

    def of_y(ref, y):
        return ref.at[:, pl.ds(pl.multiple_of(y * 160, 32), 160)]

    far = links.to(of_y(part, me.yo), r1, {"dp_0": me.yp})
    near = links.to(of_y(part, me.ym), r0, {"dp_0": me.ym})
    far.wait_recv()
    s1[...] = r1[...] + of_y(part, me.yp)[...]
    last = links.to(s1, r2, {"dp_0": me.yp})
    near.wait_recv()
    chunk[...] = r0[...] + of_y(part, me.y)[...]
    last.wait_recv()
    chunk[...] += r2[...]

    def z_rows(z):
        return z // 4, pl.multiple_of(lax.rem(z, 4) * 40, 8)

    came = []
    for k in range(1, 8):
        half, row = z_rows(me.zk(k))
        came.append(
            links.to(chunk.at[half, pl.ds(row, 40)], zr.at[k - 1], {"dp_1": me.zk(k)})
        )
    go.first()
    go.second()
    half, row = z_rows(me.z)
    for copy in came:
        copy.wait_recv()
    total = chunk[half, pl.ds(row, 40), :]
    for k in range(7):
        total += zr[k]
    zs[...] = total
    spot = full.at[half, pl.ds(pl.multiple_of(me.y * 160 + row, 8), 40)]
    came = [links.to(zs, spot, {"dp_1": me.zk(k)}) for k in range(1, 8)]
    spot[...] = total
    for copy in came:
        copy.wait_recv()
    mine = of_y(full, me.y)
    up = links.to(mine, mine, {"dp_0": me.yp})
    down = links.to(mine, mine, {"dp_0": me.ym})
    go.third()
    up.wait_recv()
    block = of_y(full, me.ym)
    far = links.to(block, block, {"dp_0": me.yp})
    go.rest()

    @pl.loop(0, 8)
    def _(n):
        cols = pl.ds(pl.multiple_of(n * 256, 256), 256)
        acc = 0.95 * buf[:, cols]
        for j in range(4):
            acc += mxu(acts_t[j], ogg[j, :, cols])
        buf[:, cols] = acc

    store = pltpu.make_async_copy(buf, buf_out, local.at[4])
    store.start()
    down.wait_recv()
    far.wait_recv()
    left_out[:, :128] = full[0]
    left_out[:, 128:] = full[1]
    store.wait()
    links.finish()


def buffer_and_left(acts, out_grad, momentum, q_basis):
    any_space = pl.BlockSpec(memory_space=pl.ANY)
    copies = 21 + 3 + 14 + 3
    scratch = [
        pltpu.VMEM((1024, 640), BF16),
        pltpu.VMEM((4, 640, 256), BF16),
        pltpu.VMEM((640, 2048), F32),
        pltpu.VMEM((8, 256, 256), F32),
        pltpu.VMEM((2048, 256), BF16),
        pltpu.VMEM((2048, 256), BF16),
        pltpu.VMEM((4, 256, 256), F32),
        pltpu.VMEM((4, 256, 256), BF16),
        pltpu.VMEM((4, 256, 256), BF16),
        pltpu.VMEM((4, 256, 2048), BF16),
        pltpu.VMEM((2, 640, 128), F32),
        pltpu.VMEM((2, 160, 128), F32),
        pltpu.VMEM((2, 160, 128), F32),
        pltpu.VMEM((2, 160, 128), F32),
        pltpu.VMEM((2, 160, 128), F32),
        pltpu.VMEM((2, 160, 128), F32),
        pltpu.VMEM((7, 40, 128), F32),
        pltpu.VMEM((40, 128), F32),
        pltpu.VMEM((2, 640, 128), F32),
        pltpu.SemaphoreType.DMA((copies,)),
        pltpu.SemaphoreType.DMA((copies,)),
        pltpu.SemaphoreType.DMA((5,)),
    ]
    return pl.pallas_call(
        left_kernel,
        out_shape=(
            jax.ShapeDtypeStruct((640, 2048), F32),
            jax.ShapeDtypeStruct((640, 256), F32),
        ),
        in_specs=[any_space] * 4,
        out_specs=(any_space, pl.BlockSpec(memory_space=pltpu.VMEM)),
        scratch_shapes=scratch,
        compiler_params=pltpu.CompilerParams(
            collective_id=0, has_side_effects=True, vmem_limit_bytes=48 * 2**20
        ),
        name="buffer_and_left",
    )(acts, out_grad, momentum, q_basis)


def from_everyone(value, axis):
    copies = jnp.broadcast_to(value, (lax.axis_size(axis), *value.shape))
    return lax.all_to_all(copies, axis, split_axis=0, concat_axis=0, tiled=True)


def in_order(blocks, dim):
    blocks = jnp.moveaxis(blocks, 0, dim)
    dims = blocks.shape
    return blocks.reshape(*dims[:dim], dims[dim] * dims[dim + 1], *dims[dim + 2 :])


def whole_of(value, axes, dim):
    far, near = axes
    blocks = from_everyone(from_everyone(value, far), near)
    return in_order(blocks.swapaxes(0, 1).reshape(-1, *value.shape), dim)


def filled_up(lines, count):
    spare = -len(lines) % count
    return jnp.pad(lines, [(0, spare)] + [(0, 0)] * (lines.ndim - 1))


def collect(value, axis, dim):
    blocks = from_everyone(value, axis)
    return in_order(blocks, dim)


def split_up(value, dim, count):
    dims = value.shape
    blocks = value.reshape(*dims[:dim], count, dims[dim] // count, *dims[dim + 1 :])
    return jnp.moveaxis(blocks, dim, 0)


def summed_on_arrival(value, axis, dim):
    blocks = split_up(value, dim, lax.axis_size(axis))
    arrived = lax.all_to_all(blocks, axis, split_axis=0, concat_axis=0, tiled=True)
    return arrived.sum(axis=0)


def sum_by_parts(value, axes):
    lines = value.reshape(-1, value.shape[-1])
    padded = filled_up(lines, lax.axis_size(axes))
    whole = collect(summed_on_arrival(padded, axes, 0), axes, 0)
    return lax.slice_in_dim(whole, 0, len(lines)).reshape(value.shape)


def of_everyone(value, axis):
    return from_everyone(value, axis).sum(axis=0)


def summed_rows(value, axes, dim):
    far, near = axes
    own = summed_on_arrival(split_up(value, dim, lax.axis_size(far)), near, dim + 1)
    return jnp.sum(lax.all_to_all(own, far, 0, 0, tiled=True), axis=0)


def sum_by_parts_2(value, axes):
    lines = value.reshape(-1, value.shape[-1])
    padded = filled_up(lines, lax.axis_size(axes[0]) * lax.axis_size(axes[1]))
    whole = whole_of(summed_rows(padded, axes, 0), axes, 0)
    return lax.slice_in_dim(whole, 0, len(lines)).reshape(value.shape)


def contract_rows(first, second):
    return lax.dot_general(
        first, second, (((0,), (0,)), ((), ())), precision=HIGH, preferred_element_type=jnp.float32
    )


def orthonormal(left, gram):
    chol = jnp.linalg.cholesky(gram)
    return lax.linalg.triangular_solve(chol, left, left_side=False, lower=True, transpose_a=True)


def body(acts, out_grad, momentum, q_basis):
    width_out = out_grad.shape[1]
    replicas = lax.axis_size(DP)
    buffer, left = buffer_and_left(acts, out_grad, momentum, q_basis)
    gram = of_everyone(contract_rows(left, left), TENSOR)
    ortho = orthonormal(left, gram)
    right = (
        sum_by_parts_2(contract_rows(buffer, ortho), (("dp_0", "dp_1"), ("tensor_0", "tensor_1")))
        / replicas
    )
    update = jnp.dot(ortho, right.T, precision=HIGH, preferred_element_type=jnp.float32)
    new_momentum = buffer - 0.05 * update
    own_rows = width_out // lax.axis_size(TENSOR)
    right_own = lax.dynamic_slice_in_dim(right, lax.axis_index(TENSOR) * own_rows, own_rows, 0)
    col_squares = jnp.sum(right * right, axis=0, keepdims=True)
    new_q = right_own * lax.rsqrt(col_squares + 1e-06)
    return (new_momentum, ortho, new_q)


def solution(mesh):
    split = Mesh(mesh.devices.reshape(4, 8, 4, 2), ("dp_0", "dp_1", "tensor_0", "tensor_1"))
    return jax.shard_map(
        body,
        mesh=split,
        in_specs=(P(DP, TENSOR), P(DP_TENSOR, None), P(DP_TENSOR, None), P(TENSOR, None)),
        out_specs=(P(DP_TENSOR, None), P(TENSOR, None), P(TENSOR, None)),
        check_vma=False,
    )
```

```python
import jax
import jax.numpy as jnp
from jax import lax
from jax.experimental import pallas as pl
from jax.experimental.pallas import tpu as pltpu
from jax.sharding import Mesh
from jax.sharding import PartitionSpec as P

DP = ("dp_0", "dp_1")
TENSOR = ("tensor_0", "tensor_1")
DP_TENSOR = ("dp_0", "dp_1", "tensor_0", "tensor_1")
HIGH = lax.Precision.HIGHEST
F32, BF16 = jnp.float32, jnp.bfloat16
MESH = pl.DeviceIdType.MESH


def halves(value):
    high = value.astype(BF16)
    return high, (value - high.astype(F32)).astype(BF16)


def mxu(a, b):
    return lax.dot_general(a, b, (((1,), (0,)), ((), ())), preferred_element_type=F32)


class Place:
    def __init__(self):
        self.y, self.z = lax.axis_index("dp_0"), lax.axis_index("dp_1")
        self.x, self.c = lax.axis_index("tensor_0"), lax.axis_index("tensor_1")
        step = 1 - 2 * self.c
        self.sib = 1 - self.c
        self.xp, self.xm = lax.rem(self.x + step + 4, 4), lax.rem(self.x - step + 4, 4)
        self.yp, self.ym = lax.rem(self.y + step + 4, 4), lax.rem(self.y - step + 4, 4)
        self.xo, self.yo = lax.rem(self.x + 2, 4), lax.rem(self.y + 2, 4)

    def tensor_peers(self):
        peers = [{"tensor_1": self.sib}]
        for n in range(1, 4):
            there = lax.rem(self.x + n, 4)
            peers.append({"tensor_0": there, "tensor_1": self.c})
            peers.append({"tensor_0": there, "tensor_1": self.sib})
        return peers

    def zk(self, k):
        return lax.rem(self.z + k, 8)


def greet(me):
    barrier = pltpu.get_barrier_semaphore()
    targets = me.tensor_peers()
    targets += [{"dp_0": me.yp}, {"dp_0": me.ym}]
    targets += [{"dp_1": me.zk(k)} for k in range(1, 8)]
    for target in targets:
        pl.semaphore_signal(barrier, inc=1, device_id=target, device_id_type=MESH)
    pl.semaphore_wait(barrier, len(targets))


class Links:
    def __init__(self, send, recv):
        self.send, self.recv, self.used, self.sent = send, recv, 0, []

    def to(self, src, dst, target):
        copy = pltpu.make_async_remote_copy(
            src_ref=src,
            dst_ref=dst,
            send_sem=self.send.at[self.used],
            recv_sem=self.recv.at[self.used],
            device_id=target,
            device_id_type=MESH,
        )
        self.used += 1
        copy.start()
        self.sent.append(copy)
        return copy

    def finish(self):
        for copy in self.sent:
            copy.wait_send()


class Gather:
    def __init__(self, me, links, own, slot):
        self.me, self.links, self.slot = me, links, slot
        here = slot(me.x, me.c)
        self.a = links.to(own, here, {"tensor_0": me.xp})
        self.b = links.to(own, here, {"tensor_0": me.xm})
        self.s0 = links.to(own, here, {"tensor_1": me.sib})

    def first(self):
        me = self.me
        self.a.wait_recv()
        block = self.slot(me.xm, me.c)
        self.f = self.links.to(block, block, {"tensor_0": me.xp})
        self.s1 = self.links.to(block, block, {"tensor_1": me.sib})

    def second(self):
        me = self.me
        self.b.wait_recv()
        block = self.slot(me.xp, me.c)
        self.s2 = self.links.to(block, block, {"tensor_1": me.sib})

    def third(self):
        me = self.me
        self.f.wait_recv()
        block = self.slot(me.xo, me.c)
        self.s3 = self.links.to(block, block, {"tensor_1": me.sib})

    def rest(self):
        for copy in (self.s0, self.s1, self.s2, self.s3):
            copy.wait_recv()


class RingSum:
    def __init__(self, links, axis, places, src, came, stage):
        own, plus, minus, far = places
        self.links, self.axis, self.src = links, axis, src
        self.own, self.plus, self.came, self.stage = own, plus, came, stage
        self.far = links.to(src(far), came.at[0], {axis: plus})
        self.near = links.to(src(minus), came.at[1], {axis: minus})

    def middle(self):
        self.far.wait_recv()
        self.stage[...] = self.came[0] + self.src(self.plus)[...]
        self.last = self.links.to(self.stage, self.came.at[2], {self.axis: self.plus})

    def total(self):
        self.near.wait_recv()
        self.last.wait_recv()
        return self.src(self.own)[...] + self.came[1] + self.came[2]


class RingSpread:
    def __init__(self, links, axis, places, slot):
        own, plus, minus, _ = places
        self.links, self.axis, self.plus = links, axis, plus
        self.from_minus = slot(minus)
        self.up = links.to(slot(own), slot(own), {axis: plus})
        self.down = links.to(slot(own), slot(own), {axis: minus})

    def middle(self):
        self.up.wait_recv()
        self.far = self.links.to(self.from_minus, self.from_minus, {self.axis: self.plus})

    def finish(self):
        self.down.wait_recv()
        self.far.wait_recv()


def three(a, b, dims=((1,), (0,))):
    dot = lambda p, q: lax.dot_general(p, q, (dims, ((), ())), preferred_element_type=F32)
    return dot(a[0], b[0]) + dot(a[0], b[1]) + dot(a[1], b[0])


def rows_at(start, size, unit=8):
    return pl.ds(pl.multiple_of(start, unit), size)


def eliminate(d):
    lane = lax.broadcasted_iota(jnp.int32, (64, 128), 1)
    row = lax.broadcasted_iota(jnp.int32, (64, 128), 0)
    e = jnp.where(lane < 64, d, jnp.where(lane - 64 == row, 1.0, 0.0).astype(F32))

    def panel(p, e):
        live = 64 - 8 * p
        for first in range(0, 8, 8):
            cols = [jnp.broadcast_to(e[:, j : j + 1], (64, 128)) for j in range(first, first + 8)]
            for n, col in enumerate(cols):
                j = first + n
                weight = pl.reciprocal(col[j : j + 1])
                factor = jnp.where((row > j) & (row < live), col, 0.0) * weight
                e = e - factor * e[j : j + 1]
                for m in range(n + 1, 8):
                    cols[m] = cols[m] - factor * col[first + m : first + m + 1]
        e = pltpu.roll(e, 120, 1)
        return jnp.concatenate([e[8:], e[:8]], axis=0)

    e = lax.fori_loop(0, 8, panel, e)
    v = e[:, :64]
    diag = jnp.sum(jnp.where(lane - 64 == row, e, 0.0), axis=1, keepdims=True)
    return v * lax.rsqrt(diag)


def exact(a, b, dims=((1,), (0,))):
    return lax.dot_general(a, b, (dims, ((), ())), precision=HIGH, preferred_element_type=F32)


def factor_block(k, a, inv):
    rows = slice(64 * k, 64 * k + 64)
    block = a[rows, 128 * (k // 2) : 128 * (k // 2) + 128]
    if k % 2:
        block = pltpu.roll(block, 64, 1)
    v = eliminate(block)
    inv_row = exact(v, inv[rows, :])
    inv[rows, :] = inv_row
    if k < 3:
        u = exact(v, a[rows, :])
        below = u.T[64 * (k + 1) :, :]
        rest = slice(64 * (k + 1), 256)
        a[rest, :] = a[rest, :] - exact(below, u)
        inv[rest, :] = inv[rest, :] - exact(below, inv_row)


def step_kernel(
    acts, og, mom, q, new_out, ortho_out, q_out,
    actsv, acts_t, buf, qg, qh, ql, yg, yh, yl, ogg,
    part, r_left, s1, chunk, zr, zs, full,
    lh, ll, lth, ltl, gram, gram_r, gram_x, gram_f, a, inv,
    cc, c_sib, c_sum, rx, sx, tx, ry, sy, ty, rxy, sxy, ryx, syx,
    rest, zr2, zs2, all_z, own_right, wide, sq, ob,
    send, recv, local,
):
    me = Place()
    links = Links(send, recv)
    own_q = qg.at[me.x * 2 + me.c]
    own_rows = pl.ds(pl.multiple_of(me.c * 128, 128), 128)
    own_og = ogg.at[me.x, own_rows]
    loads = [
        pltpu.make_async_copy(q, own_q, local.at[0]),
        pltpu.make_async_copy(og, own_og, local.at[1]),
        pltpu.make_async_copy(acts, actsv, local.at[2]),
        pltpu.make_async_copy(mom, buf, local.at[3]),
    ]
    for load in loads:
        load.start()
    greet(me)
    gq = Gather(me, links, q, lambda x, c: qg.at[x * 2 + c])
    loads[2].wait()
    for j in range(4):
        acts_t[j] = actsv[256 * j : 256 * (j + 1), :].T
    gq.first()
    gq.second()
    gq.third()
    loads[0].wait()
    gq.rest()

    @pl.loop(0, 8)
    def _(b):
        high, low = halves(qg[b])
        rows = pl.ds(pl.multiple_of(b * 256, 256), 256)
        qh[rows], ql[rows] = high, low

    loads[1].wait()
    own = ogg[me.x, own_rows, :]
    own_y = yg.at[me.x, own_rows]
    yg[me.x, own_rows, :] = mxu(own, qh[...]) + mxu(own, ql[...])
    gy = Gather(me, links, own_y, lambda x, c: yg.at[x, pl.ds(pl.multiple_of(c * 128, 128), 128)])
    loads[3].wait()

    def momentum_part(t):
        rows = pl.ds(pl.multiple_of(t * 128, 128), 128)
        high, low = halves(buf[rows, :])
        acc = mxu(high, qh[...]) + mxu(high, ql[...]) + mxu(low, qh[...])
        acc = acc * (0.95 / 32)
        part[0, rows, :] = acc[:, :128]
        part[1, rows, :] = acc[:, 128:]

    pl.loop(0, 2)(momentum_part)
    gy.first()
    gy.second()
    pl.loop(2, 5)(momentum_part)
    gy.third()
    gy.rest()
    go = Gather(
        me, links, og, lambda x, c: ogg.at[x, pl.ds(pl.multiple_of(c * 128, 128), 128)]
    )
    for j in range(4):
        high, low = halves(yg[j])
        yh[j], yl[j] = high, low

    @pl.loop(0, 5)
    def _(t):
        rows = pl.ds(pl.multiple_of(t * 128, 128), 128)
        acc = jnp.zeros((128, 256), F32)
        for j in range(4):
            lhs = acts_t[j, rows, :]
            acc += mxu(lhs, yh[j]) + mxu(lhs, yl[j])
        acc = acc * (1 / 32)
        part[0, rows, :] += acc[:, :128]
        part[1, rows, :] += acc[:, 128:]

    def of_y(ref, y):
        return ref.at[:, pl.ds(pl.multiple_of(y * 160, 32), 160)]

    ys, xs = (me.y, me.yp, me.ym, me.yo), (me.x, me.xp, me.xm, me.xo)
    ring = RingSum(links, "dp_0", ys, lambda y: of_y(part, y), r_left, s1)
    ring.middle()
    chunk[...] = ring.total()

    def z_rows(z):
        return z // 4, pl.multiple_of(lax.rem(z, 4) * 40, 8)

    came = []
    for k in range(1, 8):
        half, row = z_rows(me.zk(k))
        came.append(
            links.to(chunk.at[half, pl.ds(row, 40)], zr.at[k - 1], {"dp_1": me.zk(k)})
        )
    go.first()
    go.second()
    half, row = z_rows(me.z)
    for copy in came:
        copy.wait_recv()
    total = chunk[half, pl.ds(row, 40), :]
    for k in range(7):
        total += zr[k]
    zs[...] = total
    spot = full.at[half, pl.ds(pl.multiple_of(me.y * 160 + row, 8), 40)]
    came = [links.to(zs, spot, {"dp_1": me.zk(k)}) for k in range(1, 8)]
    spot[...] = total
    for copy in came:
        copy.wait_recv()
    spread = RingSpread(links, "dp_0", ys, lambda y: of_y(full, y))
    go.third()
    spread.middle()
    go.rest()

    @pl.loop(0, 8)
    def _(n):
        cols = pl.ds(pl.multiple_of(n * 256, 256), 256)
        acc = 0.95 * buf[:, cols]
        for j in range(4):
            acc += mxu(acts_t[j], ogg[j, :, cols])
        buf[:, cols] = acc

    spread.finish()
    for half in range(2):
        cols = slice(128 * half, 128 * half + 128)
        lh[:, cols], ll[:, cols] = halves(full[half])
        lth[cols, :], ltl[cols, :] = halves(full[half].T)

    gram[...] = three((lth[...], ltl[...]), (lh[...], ll[...]))
    pair = links.to(gram, gram_r, {"tensor_1": me.sib})

    def product_with(core):
        @pl.loop(0, 4)
        def _(n):
            cols = rows_at((2 * n + core) * 256, 256, 256)
            block = three((lth[...], ltl[...]), halves(buf[:, cols]))
            cc[n, core] = block.T

    product_with(me.sib)
    swap = links.to(cc.at[:, me.sib], c_sib, {"tensor_1": me.sib})
    pair.wait_recv()
    half_rows = rows_at(me.c * 128, 128)
    gram_x[me.x] = gram[half_rows, :] + gram_r[half_rows, :]
    gram_spread = RingSpread(links, "tensor_0", xs, lambda x: gram_x.at[x])
    product_with(me.c)
    gram_spread.middle()
    swap.wait_recv()
    c_sum[...] = cc[:, me.c].reshape(4, 2, 128, 256) + c_sib[...].reshape(4, 2, 128, 256)
    x_first = RingSum(links, "tensor_0", xs, lambda x: c_sum.at[x, 0], rx, sx)
    y_first = RingSum(
        links, "dp_0", ys, lambda y: c_sum.at[:, 1, rows_at(y * 32, 32)], ry, sy
    )
    gram_spread.finish()
    gram_f[me.c] = ((gram_x[0] + gram_x[1]) + gram_x[2]) + gram_x[3]
    here = gram_f.at[me.c]
    whole = links.to(here, here, {"tensor_1": me.sib})
    same = lax.broadcasted_iota(jnp.int32, (256, 256), 0) == lax.broadcasted_iota(
        jnp.int32, (256, 256), 1
    )
    inv[...] = jnp.where(same, 1.0, 0.0).astype(F32)
    y_first.middle()
    x_first.middle()
    whole.wait_recv()
    a[:128, :] = gram_f[0]
    a[128:, :] = gram_f[1]

    factor_block(0, a, inv)
    tx[...] = x_first.total()
    then_y = RingSum(links, "dp_0", ys, lambda y: tx.at[rows_at(y * 32, 32)], ryx, syx)
    ty[...] = y_first.total()
    then_x = RingSum(links, "tensor_0", xs, lambda x: ty.at[x], rxy, sxy)
    factor_block(1, a, inv)
    then_y.middle()
    then_x.middle()
    factor_block(2, a, inv)
    rest[:32, :] = then_y.total()
    rest[32:, :] = then_x.total()
    came = [
        links.to(rest.at[rows_at(me.zk(k) * 8, 8)], zr2.at[k - 1], {"dp_1": me.zk(k)})
        for k in range(1, 8)
    ]
    factor_block(3, a, inv)
    for copy in came:
        copy.wait_recv()
    total = rest[rows_at(me.z * 8, 8), :]
    for k in range(7):
        total += zr2[k]
    total = total * (1 / 32)
    zs2[...] = total
    spot = all_z.at[rows_at(me.z * 8, 8)]
    came = [links.to(zs2, spot, {"dp_1": me.zk(k)}) for k in range(1, 8)]
    spot[...] = total
    inverse = halves(inv[...])
    across = ((1,), (1,))
    for copy in came:
        copy.wait_recv()
    mine = three(halves(all_z[...]), inverse, across)
    own_right[0, rows_at(me.y * 32, 32), :] = mine[:32]
    own_right[1, rows_at(me.y * 32, 32), :] = mine[32:]
    right_y = RingSpread(
        links, "dp_0", ys, lambda y: own_right.at[:, rows_at(y * 32, 32)]
    )
    ortho = three((lh[...], ll[...]), inverse, across)
    ortho_out[...] = ortho
    ob[...] = (ortho * 0.05).astype(BF16)
    right_y.middle()
    right_y.finish()
    index = 2 * me.x + me.c
    wide[index, :128, :] = own_right[0].astype(BF16)
    wide[index, 128:, :] = own_right[1].astype(BF16)
    gw = Gather(me, links, wide.at[index], lambda x, c: wide.at[2 * x + c])
    values = own_right[...].reshape(256, 256)
    sq[index] = jnp.broadcast_to(jnp.sum(values * values, axis=0, keepdims=True), (8, 256))
    mark = sq.at[index]
    came = [links.to(mark, mark, peer) for peer in me.tensor_peers()]
    stores = []

    def finish_block(x, c):
        cols = rows_at((2 * x + c) * 256, 256, 256)
        update = lax.dot_general(
            ob[...], wide[2 * x + c], (across, ((), ())), preferred_element_type=F32
        )
        buf[:, cols] = buf[:, cols] - update
        store = pltpu.make_async_copy(
            buf.at[:, cols], new_out.at[:, cols], local.at[4 + len(stores)]
        )
        store.start()
        stores.append(store)

    finish_block(me.x, me.c)
    gw.first()
    finish_block(me.xm, me.c)
    gw.second()
    finish_block(me.xp, me.c)
    gw.s0.wait_recv()
    finish_block(me.x, me.sib)
    gw.third()
    finish_block(me.xo, me.c)
    gw.s1.wait_recv()
    finish_block(me.xp, me.sib)
    gw.s2.wait_recv()
    finish_block(me.xm, me.sib)
    for copy in came:
        copy.wait_recv()
    squares = sq[0]
    for b in range(1, 8):
        squares += sq[b]
    q_out[...] = values * lax.rsqrt(squares[:1] + 1e-06)
    gw.s3.wait_recv()
    finish_block(me.xo, me.sib)
    for store in stores:
        store.wait()
    links.finish()


def whole_step(acts, out_grad, momentum, q_basis):
    any_space = pl.BlockSpec(memory_space=pl.ANY)
    in_vmem = pl.BlockSpec(memory_space=pltpu.VMEM)
    copies = 120
    vm = pltpu.VMEM
    scratch = [
        vm((1024, 640), BF16),
        vm((4, 640, 256), BF16),
        vm((640, 2048), F32),
        vm((8, 256, 256), F32),
        vm((2048, 256), BF16),
        vm((2048, 256), BF16),
        vm((4, 256, 256), F32),
        vm((4, 256, 256), BF16),
        vm((4, 256, 256), BF16),
        vm((4, 256, 2048), BF16),
        vm((2, 640, 128), F32),
        vm((3, 2, 160, 128), F32),
        vm((2, 160, 128), F32),
        vm((2, 160, 128), F32),
        vm((7, 40, 128), F32),
        vm((40, 128), F32),
        vm((2, 640, 128), F32),
        vm((640, 256), BF16),
        vm((640, 256), BF16),
        vm((256, 640), BF16),
        vm((256, 640), BF16),
        vm((256, 256), F32),
        vm((256, 256), F32),
        vm((4, 128, 256), F32),
        vm((2, 128, 256), F32),
        vm((256, 256), F32),
        vm((256, 256), F32),
        vm((4, 2, 256, 256), F32),
        vm((4, 256, 256), F32),
        vm((4, 2, 128, 256), F32),
        vm((3, 128, 256), F32),
        vm((128, 256), F32),
        vm((128, 256), F32),
        vm((3, 4, 32, 256), F32),
        vm((4, 32, 256), F32),
        vm((4, 32, 256), F32),
        vm((3, 32, 256), F32),
        vm((32, 256), F32),
        vm((3, 32, 256), F32),
        vm((32, 256), F32),
        vm((64, 256), F32),
        vm((7, 8, 256), F32),
        vm((8, 256), F32),
        vm((64, 256), F32),
        vm((2, 128, 256), F32),
        vm((8, 256, 256), BF16),
        vm((8, 8, 256), F32),
        vm((640, 256), BF16),
        pltpu.SemaphoreType.DMA((copies,)),
        pltpu.SemaphoreType.DMA((copies,)),
        pltpu.SemaphoreType.DMA((12,)),
    ]
    return pl.pallas_call(
        step_kernel,
        out_shape=(
            jax.ShapeDtypeStruct((640, 2048), F32),
            jax.ShapeDtypeStruct((640, 256), F32),
            jax.ShapeDtypeStruct((256, 256), F32),
        ),
        in_specs=[any_space] * 4,
        out_specs=(any_space, in_vmem, in_vmem),
        scratch_shapes=scratch,
        compiler_params=pltpu.CompilerParams(
            collective_id=0, has_side_effects=True, vmem_limit_bytes=60 * 2**20
        ),
        name="whole_step",
    )(acts, out_grad, momentum, q_basis)


def solution(mesh):
    split = Mesh(mesh.devices.reshape(4, 8, 4, 2), ("dp_0", "dp_1", "tensor_0", "tensor_1"))
    return jax.shard_map(
        whole_step,
        mesh=split,
        in_specs=(P(DP, TENSOR), P(DP_TENSOR, None), P(DP_TENSOR, None), P(TENSOR, None)),
        out_specs=(P(DP_TENSOR, None), P(TENSOR, None), P(TENSOR, None)),
        check_vma=False,
    )
```

```python
import jax
import jax.numpy as jnp
from jax import lax
from jax.experimental import pallas as pl
from jax.experimental.pallas import tpu as pltpu
from jax.sharding import Mesh
from jax.sharding import PartitionSpec as P

DP = ("dp_0", "dp_1")
TENSOR = ("tensor_0", "tensor_1")
DP_TENSOR = ("dp_0", "dp_1", "tensor_0", "tensor_1")
HIGH = lax.Precision.HIGHEST
F32, BF16 = jnp.float32, jnp.bfloat16
MESH = pl.DeviceIdType.MESH


def halves(value):
    high = value.astype(BF16)
    return high, (value - high.astype(F32)).astype(BF16)


def mxu(a, b):
    return lax.dot_general(a, b, (((1,), (0,)), ((), ())), preferred_element_type=F32)


class Place:
    def __init__(self):
        self.y, self.z = lax.axis_index("dp_0"), lax.axis_index("dp_1")
        self.x, self.c = lax.axis_index("tensor_0"), lax.axis_index("tensor_1")
        step = 1 - 2 * self.c
        self.sib = 1 - self.c
        self.xp, self.xm = lax.rem(self.x + step + 4, 4), lax.rem(self.x - step + 4, 4)
        self.yp, self.ym = lax.rem(self.y + step + 4, 4), lax.rem(self.y - step + 4, 4)
        self.xo, self.yo = lax.rem(self.x + 2, 4), lax.rem(self.y + 2, 4)

    def tensor_peers(self):
        peers = [({"tensor_1": self.sib}, 2 * self.x + self.sib)]
        for n in range(1, 4):
            there = lax.rem(self.x + n, 4)
            for core in (self.c, self.sib):
                peers.append(({"tensor_0": there, "tensor_1": core}, 2 * there + core))
        return peers

    def zk(self, k):
        return lax.rem(self.z + k, 8)


def greet(me):
    barrier = pltpu.get_barrier_semaphore()
    targets = [peer for peer, _ in me.tensor_peers()]
    targets += [{"dp_0": me.yp}, {"dp_0": me.ym}]
    targets += [{"dp_1": me.zk(k)} for k in range(1, 8)]
    for target in targets:
        pl.semaphore_signal(barrier, inc=1, device_id=target, device_id_type=MESH)
    pl.semaphore_wait(barrier, len(targets))


class Links:
    def __init__(self, send, recv):
        self.send, self.recv, self.used, self.sent = send, recv, 0, []

    def to(self, src, dst, target):
        copy = pltpu.make_async_remote_copy(
            src_ref=src,
            dst_ref=dst,
            send_sem=self.send.at[self.used],
            recv_sem=self.recv.at[self.used],
            device_id=target,
            device_id_type=MESH,
        )
        self.used += 1
        copy.start()
        self.sent.append(copy)
        return copy

    def finish(self):
        for copy in self.sent:
            copy.wait_send()


class Gather:
    def __init__(self, me, links, own, slot):
        self.me, self.links, self.slot = me, links, slot
        here = slot(me.x, me.c)
        self.a = links.to(own, here, {"tensor_0": me.xp})
        self.b = links.to(own, here, {"tensor_0": me.xm})
        self.s0 = links.to(own, here, {"tensor_1": me.sib})

    def first(self):
        me = self.me
        self.a.wait_recv()
        block = self.slot(me.xm, me.c)
        self.f = self.links.to(block, block, {"tensor_0": me.xp})
        self.s1 = self.links.to(block, block, {"tensor_1": me.sib})

    def second(self):
        me = self.me
        self.b.wait_recv()
        block = self.slot(me.xp, me.c)
        self.s2 = self.links.to(block, block, {"tensor_1": me.sib})

    def third(self):
        me = self.me
        self.f.wait_recv()
        block = self.slot(me.xo, me.c)
        self.s3 = self.links.to(block, block, {"tensor_1": me.sib})

    def rest(self):
        for copy in (self.s0, self.s1, self.s2, self.s3):
            copy.wait_recv()


class RingSum:
    def __init__(self, links, axis, places, src, came, stage):
        own, plus, minus, far = places
        self.links, self.axis, self.src = links, axis, src
        self.own, self.plus, self.came, self.stage = own, plus, came, stage
        self.far = links.to(src(far), came.at[0], {axis: plus})
        self.near = links.to(src(minus), came.at[1], {axis: minus})

    def middle(self):
        self.far.wait_recv()
        self.stage[...] = self.came[0] + self.src(self.plus)[...]
        self.last = self.links.to(self.stage, self.came.at[2], {self.axis: self.plus})

    def total(self):
        self.near.wait_recv()
        self.last.wait_recv()
        return self.src(self.own)[...] + self.came[1] + self.came[2]


class RingSpread:
    def __init__(self, links, axis, places, slot):
        own, plus, minus, _ = places
        self.links, self.axis, self.plus = links, axis, plus
        self.from_minus = slot(minus)
        self.up = links.to(slot(own), slot(own), {axis: plus})
        self.down = links.to(slot(own), slot(own), {axis: minus})

    def middle(self):
        self.up.wait_recv()
        self.far = self.links.to(self.from_minus, self.from_minus, {self.axis: self.plus})

    def finish(self):
        self.down.wait_recv()
        self.far.wait_recv()


def three(a, b, dims=((1,), (0,))):
    dot = lambda p, q: lax.dot_general(p, q, (dims, ((), ())), preferred_element_type=F32)
    return dot(a[0], b[0]) + dot(a[0], b[1]) + dot(a[1], b[0])


def rows_at(start, size, unit=8):
    return pl.ds(pl.multiple_of(start, unit), size)


def eliminate(d):
    lane = lax.broadcasted_iota(jnp.int32, (64, 128), 1)
    row = lax.broadcasted_iota(jnp.int32, (64, 128), 0)
    e = jnp.where(lane < 64, d, jnp.where(lane - 64 == row, 1.0, 0.0).astype(F32))

    def panel(p, e):
        live = 64 - 8 * p
        for first in range(0, 8, 8):
            cols = [jnp.broadcast_to(e[:, j : j + 1], (64, 128)) for j in range(first, first + 8)]
            for n, col in enumerate(cols):
                j = first + n
                weight = pl.reciprocal(col[j : j + 1])
                factor = jnp.where((row > j) & (row < live), col, 0.0) * weight
                e = e - factor * e[j : j + 1]
                for m in range(n + 1, 8):
                    cols[m] = cols[m] - factor * col[first + m : first + m + 1]
        e = pltpu.roll(e, 120, 1)
        return jnp.concatenate([e[8:], e[:8]], axis=0)

    e = lax.fori_loop(0, 8, panel, e)
    v = e[:, :64]
    diag = jnp.sum(jnp.where(lane - 64 == row, e, 0.0), axis=1, keepdims=True)
    return v * lax.rsqrt(diag)


def exact(a, b, dims=((1,), (0,))):
    return lax.dot_general(a, b, (dims, ((), ())), precision=HIGH, preferred_element_type=F32)


def factor_block(k, a, inv):
    rows = slice(64 * k, 64 * k + 64)
    block = a[rows, 128 * (k // 2) : 128 * (k // 2) + 128]
    if k % 2:
        block = pltpu.roll(block, 64, 1)
    v = eliminate(block)
    inv_row = exact(v, inv[rows, :])
    inv[rows, :] = inv_row
    if k < 3:
        u = exact(v, a[rows, :])
        below = u.T[64 * (k + 1) :, :]
        rest = slice(64 * (k + 1), 256)
        a[rest, :] = a[rest, :] - exact(below, u)
        inv[rest, :] = inv[rest, :] - exact(below, inv_row)


def step_kernel(
    acts, og, mom, q, buf_out, ob, wide_out, ortho_out, q_out,
    actsv, acts_t, buf, qg, qh, ql, yg, yh, yl, ogg, y_own,
    part, r_left, s1, chunk, zr, zs, full,
    bth, btl, lh, ll, gram, gram_r, gram_s, a, inv,
    cc, c_sib, c_sum, rx, sx, tx, ry, sy, ty, rxy, sxy, ryx, syx,
    rest, zr2, zs2, all_z, own_right, wide, sq,
    send, recv, local,
):
    me = Place()
    links = Links(send, recv)
    own_q = qg.at[me.x * 2 + me.c]
    own_rows = pl.ds(pl.multiple_of(me.c * 128, 128), 128)
    own_og = ogg.at[me.x, own_rows]
    loads = [
        pltpu.make_async_copy(q, own_q, local.at[0]),
        pltpu.make_async_copy(og, own_og, local.at[1]),
        pltpu.make_async_copy(acts, actsv, local.at[2]),
        pltpu.make_async_copy(mom, buf, local.at[3]),
    ]
    for load in loads:
        load.start()
    greet(me)
    gq = Gather(me, links, q, lambda x, c: qg.at[x * 2 + c])
    loads[2].wait()
    for j in range(4):
        acts_t[j] = actsv[256 * j : 256 * (j + 1), :].T
    loads[0].wait()
    loads[1].wait()
    loads[3].wait()
    own = ogg.at[me.x, own_rows]

    def og_times(b, first=False):
        high, low = halves(qg[b])
        qh[b], ql[b] = high, low
        lhs = own[:, rows_at(b * 256, 256, 256)]
        share = mxu(lhs, high) + mxu(lhs, low)
        y_own[...] = share if first else y_own[...] + share

    def momentum_times(b, first=False):
        @pl.loop(0, 5)
        def _(t):
            rows = rows_at(t * 128, 128)
            share = three(halves(buf[rows, rows_at(b * 256, 256, 256)]), (qh[b], ql[b]))
            for half in range(2):
                piece = share[:, 128 * half : 128 * half + 128]
                part[half, rows, :] = piece if first else part[half, rows, :] + piece

    def take(x, c, first=False):
        og_times(2 * x + c, first)
        momentum_times(2 * x + c, first)

    take(me.x, me.c, True)
    gq.first()
    gq.second()
    gq.s0.wait_recv()
    take(me.x, me.sib)
    take(me.xm, me.c)
    take(me.xp, me.c)
    gq.s1.wait_recv()
    take(me.xp, me.sib)
    gq.s2.wait_recv()
    take(me.xm, me.sib)
    gq.third()
    take(me.xo, me.c)
    gq.s3.wait_recv()
    og_times(2 * me.xo + me.sib)
    yg[me.x, own_rows, :] = y_own[...]
    own_y = yg.at[me.x, own_rows]
    gy = Gather(me, links, own_y, lambda x, c: yg.at[x, pl.ds(pl.multiple_of(c * 128, 128), 128)])
    momentum_times(2 * me.xo + me.sib)
    gy.first()
    gy.second()
    gy.third()
    gy.rest()
    go = Gather(
        me, links, og, lambda x, c: ogg.at[x, pl.ds(pl.multiple_of(c * 128, 128), 128)]
    )
    for j in range(4):
        high, low = halves(yg[j])
        yh[j], yl[j] = high, low

    @pl.loop(0, 5)
    def _(t):
        rows = pl.ds(pl.multiple_of(t * 128, 128), 128)
        acc = jnp.zeros((128, 256), F32)
        for j in range(4):
            lhs = acts_t[j, rows, :]
            acc += mxu(lhs, yh[j]) + mxu(lhs, yl[j])
        for half in range(2):
            piece = acc[:, 128 * half : 128 * half + 128]
            part[half, rows, :] = (0.95 * part[half, rows, :] + piece) * (1 / 32)

    def of_y(ref, y):
        return ref.at[:, pl.ds(pl.multiple_of(y * 160, 32), 160)]

    ys, xs = (me.y, me.yp, me.ym, me.yo), (me.x, me.xp, me.xm, me.xo)
    ring = RingSum(links, "dp_0", ys, lambda y: of_y(part, y), r_left, s1)
    ring.middle()
    chunk[...] = ring.total()

    def z_rows(z):
        return z // 4, pl.multiple_of(lax.rem(z, 4) * 40, 8)

    came = []
    for k in range(1, 8):
        half, row = z_rows(me.zk(k))
        came.append(
            links.to(chunk.at[half, pl.ds(row, 40)], zr.at[k - 1], {"dp_1": me.zk(k)})
        )
    go.first()
    go.second()
    half, row = z_rows(me.z)
    for copy in came:
        copy.wait_recv()
    total = chunk[half, pl.ds(row, 40), :]
    for k in range(7):
        total += zr[k]
    zs[...] = total
    spot = full.at[half, pl.ds(pl.multiple_of(me.y * 160 + row, 8), 40)]
    came = [links.to(zs, spot, {"dp_1": me.zk(k)}) for k in range(1, 8)]
    spot[...] = total
    go.third()
    go.rest()

    @pl.loop(0, 8)
    def _(n):
        cols = rows_at(n * 256, 256, 256)
        acc = 0.95 * buf[:, cols]
        for j in range(4):
            acc += mxu(acts_t[j], ogg[j, :, cols])
        buf[:, cols] = acc
        for j in range(4):
            bth[j, cols, :], btl[j, cols, :] = halves(acc[160 * j : 160 * j + 160].T)

    store = pltpu.make_async_copy(buf, buf_out, local.at[4])
    store.start()
    for copy in came:
        copy.wait_recv()

    def take_left(j, first=False):
        chunk_rows = rows_at(j * 160, 160, 32)
        rows = jnp.concatenate([full[0, chunk_rows, :], full[1, chunk_rows, :]], axis=1)
        pair = halves(rows)
        lh[j], ll[j] = pair
        share = three(halves(rows.T), pair)
        gram[...] = share if first else gram[...] + share

    def product_with(core, j, first=False):
        @pl.loop(0, 4)
        def _(n):
            cols = rows_at((2 * n + core) * 256, 256, 256)
            share = three((bth[j, cols, :], btl[j, cols, :]), (lh[j], ll[j]))
            cc[n, core] = share if first else cc[n, core] + share

    spread = RingSpread(links, "dp_0", ys, lambda y: of_y(full, y))
    take_left(me.y, True)
    product_with(me.sib, me.y, True)
    spread.middle()
    product_with(me.c, me.y, True)
    take_left(me.ym)
    spread.down.wait_recv()
    take_left(me.yp)
    for core in (me.sib, me.c):
        product_with(core, me.ym)
        product_with(core, me.yp)
    spread.far.wait_recv()
    take_left(me.yo)
    index = 2 * me.x + me.c
    gram_in = []
    for peer, there in me.tensor_peers():
        gram_in.append(links.to(gram.at[rows_at(there * 32, 32)], gram_r.at[index], peer))
    gram_r[index] = gram[rows_at(index * 32, 32), :]
    product_with(me.sib, me.yo)
    swap = links.to(cc.at[:, me.sib], c_sib, {"tensor_1": me.sib})
    for copy in gram_in:
        copy.wait_recv()
    total = gram_r[0]
    for b in range(1, 8):
        total += gram_r[b]
    gram_s[...] = total
    gram_rows = a.at[rows_at(index * 32, 32)]
    gram_in = [links.to(gram_s, gram_rows, peer) for peer, _ in me.tensor_peers()]
    gram_rows[...] = total
    product_with(me.c, me.yo)
    swap.wait_recv()
    c_sum[...] = cc[:, me.c].reshape(4, 2, 128, 256) + c_sib[...].reshape(4, 2, 128, 256)
    x_first = RingSum(links, "tensor_0", xs, lambda x: c_sum.at[x, 0], rx, sx)
    y_first = RingSum(
        links, "dp_0", ys, lambda y: c_sum.at[:, 1, rows_at(y * 32, 32)], ry, sy
    )
    same = lax.broadcasted_iota(jnp.int32, (256, 256), 0) == lax.broadcasted_iota(
        jnp.int32, (256, 256), 1
    )
    inv[...] = jnp.where(same, 1.0, 0.0).astype(F32)
    y_first.middle()
    x_first.middle()
    for copy in gram_in:
        copy.wait_recv()

    factor_block(0, a, inv)
    tx[...] = x_first.total()
    then_y = RingSum(links, "dp_0", ys, lambda y: tx.at[rows_at(y * 32, 32)], ryx, syx)
    ty[...] = y_first.total()
    then_x = RingSum(links, "tensor_0", xs, lambda x: ty.at[x], rxy, sxy)
    factor_block(1, a, inv)
    then_y.middle()
    then_x.middle()
    factor_block(2, a, inv)
    rest[:32, :] = then_y.total()
    rest[32:, :] = then_x.total()
    came = [
        links.to(rest.at[rows_at(me.zk(k) * 8, 8)], zr2.at[k - 1], {"dp_1": me.zk(k)})
        for k in range(1, 8)
    ]
    factor_block(3, a, inv)
    for copy in came:
        copy.wait_recv()
    total = rest[rows_at(me.z * 8, 8), :]
    for k in range(7):
        total += zr2[k]
    total = total * (1 / 32)
    zs2[...] = total
    spot = all_z.at[rows_at(me.z * 8, 8)]
    came = [links.to(zs2, spot, {"dp_1": me.zk(k)}) for k in range(1, 8)]
    spot[...] = total
    inverse = halves(inv[...])
    across = ((1,), (1,))
    for copy in came:
        copy.wait_recv()
    mine = three(halves(all_z[...]), inverse, across)
    own_right[0, rows_at(me.y * 32, 32), :] = mine[:32]
    own_right[1, rows_at(me.y * 32, 32), :] = mine[32:]
    right_y = RingSpread(
        links, "dp_0", ys, lambda y: own_right.at[:, rows_at(y * 32, 32)]
    )
    ortho = three((lh[...].reshape(640, 256), ll[...].reshape(640, 256)), inverse, across)
    ortho_out[...] = ortho
    ob[...] = (ortho * 0.05).astype(BF16)
    right_y.middle()
    right_y.finish()
    wide[index, :128, :] = own_right[0].astype(BF16)
    wide[index, 128:, :] = own_right[1].astype(BF16)
    gw = Gather(me, links, wide.at[index], lambda x, c: wide.at[2 * x + c])
    values = own_right[...].reshape(256, 256)
    sq[index] = jnp.broadcast_to(jnp.sum(values * values, axis=0, keepdims=True), (8, 256))
    mark = sq.at[index]
    came = [links.to(mark, mark, peer) for peer, _ in me.tensor_peers()]
    gw.first()
    gw.second()
    for copy in came:
        copy.wait_recv()
    squares = sq[0]
    for b in range(1, 8):
        squares += sq[b]
    q_out[...] = values * lax.rsqrt(squares[:1] + 1e-06)
    gw.third()
    gw.rest()
    wide_out[...] = wide[...]
    store.wait()
    links.finish()


def apply_kernel(buf, ob, wide, ortho, q, new_out, ortho_out, q_out):
    lhs = ob[...]
    for b in range(8):
        cols = slice(256 * b, 256 * b + 256)
        update = lax.dot_general(
            lhs, wide[b], (((1,), (1,)), ((), ())), preferred_element_type=F32
        )
        new_out[:, cols] = buf[:, cols] - update
    ortho_out[...] = ortho[...]
    q_out[...] = q[...]


def apply_update(buf, ob, wide, ortho, q):
    def tile(rows, cols):
        return pl.BlockSpec((rows, cols), lambda i: (i, 0))

    return pl.pallas_call(
        apply_kernel,
        grid=(4,),
        out_shape=(
            jax.ShapeDtypeStruct((640, 2048), F32),
            jax.ShapeDtypeStruct((640, 256), F32),
            jax.ShapeDtypeStruct((256, 256), F32),
        ),
        in_specs=[
            tile(160, 2048),
            tile(160, 256),
            pl.BlockSpec((8, 256, 256), lambda i: (0, 0, 0)),
            tile(160, 256),
            tile(64, 256),
        ],
        out_specs=(tile(160, 2048), tile(160, 256), tile(64, 256)),
        compiler_params=pltpu.CompilerParams(vmem_limit_bytes=56 * 2**20),
        name="apply_update",
    )(buf, ob, wide, ortho, q)


def whole_step(acts, out_grad, momentum, q_basis):
    any_space = pl.BlockSpec(memory_space=pl.ANY)
    in_hbm = pl.BlockSpec(memory_space=pltpu.HBM)
    in_vmem = pl.BlockSpec(memory_space=pltpu.VMEM)
    copies = 120
    vm = pltpu.VMEM
    scratch = [
        vm((1024, 640), BF16),
        vm((4, 640, 256), BF16),
        vm((640, 2048), F32),
        vm((8, 256, 256), F32),
        vm((8, 256, 256), BF16),
        vm((8, 256, 256), BF16),
        vm((4, 256, 256), F32),
        vm((4, 256, 256), BF16),
        vm((4, 256, 256), BF16),
        vm((4, 256, 2048), BF16),
        vm((128, 256), F32),
        vm((2, 640, 128), F32),
        vm((3, 2, 160, 128), F32),
        vm((2, 160, 128), F32),
        vm((2, 160, 128), F32),
        vm((7, 40, 128), F32),
        vm((40, 128), F32),
        vm((2, 640, 128), F32),
        vm((4, 2048, 160), BF16),
        vm((4, 2048, 160), BF16),
        vm((4, 160, 256), BF16),
        vm((4, 160, 256), BF16),
        vm((256, 256), F32),
        vm((8, 32, 256), F32),
        vm((32, 256), F32),
        vm((256, 256), F32),
        vm((256, 256), F32),
        vm((4, 2, 256, 256), F32),
        vm((4, 256, 256), F32),
        vm((4, 2, 128, 256), F32),
        vm((3, 128, 256), F32),
        vm((128, 256), F32),
        vm((128, 256), F32),
        vm((3, 4, 32, 256), F32),
        vm((4, 32, 256), F32),
        vm((4, 32, 256), F32),
        vm((3, 32, 256), F32),
        vm((32, 256), F32),
        vm((3, 32, 256), F32),
        vm((32, 256), F32),
        vm((64, 256), F32),
        vm((7, 8, 256), F32),
        vm((8, 256), F32),
        vm((64, 256), F32),
        vm((2, 128, 256), F32),
        vm((8, 256, 256), BF16),
        vm((8, 8, 256), F32),
        pltpu.SemaphoreType.DMA((copies,)),
        pltpu.SemaphoreType.DMA((copies,)),
        pltpu.SemaphoreType.DMA((12,)),
    ]
    outs = pl.pallas_call(
        step_kernel,
        out_shape=(
            jax.ShapeDtypeStruct((640, 2048), F32),
            jax.ShapeDtypeStruct((640, 256), BF16),
            jax.ShapeDtypeStruct((8, 256, 256), BF16),
            jax.ShapeDtypeStruct((640, 256), F32),
            jax.ShapeDtypeStruct((256, 256), F32),
        ),
        in_specs=[in_hbm] * 4,
        out_specs=(any_space, in_vmem, in_vmem, in_vmem, in_vmem),
        scratch_shapes=scratch,
        compiler_params=pltpu.CompilerParams(
            collective_id=0, has_side_effects=True, vmem_limit_bytes=60 * 2**20
        ),
        name="whole_step",
    )(acts, out_grad, momentum, q_basis)
    return apply_update(*outs)


def solution(mesh):
    split = Mesh(mesh.devices.reshape(4, 8, 4, 2), ("dp_0", "dp_1", "tensor_0", "tensor_1"))
    return jax.shard_map(
        whole_step,
        mesh=split,
        in_specs=(P(DP, TENSOR), P(DP_TENSOR, None), P(DP_TENSOR, None), P(TENSOR, None)),
        out_specs=(P(DP_TENSOR, None), P(TENSOR, None), P(TENSOR, None)),
        check_vma=False,
    )
```

```python
import jax
import jax.numpy as jnp
from jax import lax
from jax.experimental import pallas as pl
from jax.experimental.pallas import tpu as pltpu
from jax.sharding import Mesh
from jax.sharding import PartitionSpec as P

DP = ("dp_0", "dp_1")
TENSOR = ("tensor_0", "tensor_1")
DP_TENSOR = ("dp_0", "dp_1", "tensor_0", "tensor_1")
HIGH = lax.Precision.HIGHEST
F32, BF16 = jnp.float32, jnp.bfloat16
MESH = pl.DeviceIdType.MESH


def halves(value):
    high = value.astype(BF16)
    return high, (value - high.astype(F32)).astype(BF16)


def mxu(a, b):
    return lax.dot_general(a, b, (((1,), (0,)), ((), ())), preferred_element_type=F32)


class Place:
    def __init__(self):
        self.y, self.z = lax.axis_index("dp_0"), lax.axis_index("dp_1")
        self.x, self.c = lax.axis_index("tensor_0"), lax.axis_index("tensor_1")
        step = 1 - 2 * self.c
        self.sib = 1 - self.c
        self.xp, self.xm = lax.rem(self.x + step + 4, 4), lax.rem(self.x - step + 4, 4)
        self.yp, self.ym = lax.rem(self.y + step + 4, 4), lax.rem(self.y - step + 4, 4)
        self.xo, self.yo = lax.rem(self.x + 2, 4), lax.rem(self.y + 2, 4)

    def tensor_peers(self):
        peers = [({"tensor_1": self.sib}, 2 * self.x + self.sib)]
        for n in range(1, 4):
            there = lax.rem(self.x + n, 4)
            for core in (self.c, self.sib):
                peers.append(({"tensor_0": there, "tensor_1": core}, 2 * there + core))
        return peers

    def zk(self, k):
        return lax.rem(self.z + k, 8)


def greet(me):
    barrier = pltpu.get_barrier_semaphore()
    targets = [peer for peer, _ in me.tensor_peers()]
    targets += [{"dp_0": me.yp}, {"dp_0": me.ym}]
    targets += [{"dp_1": me.zk(k)} for k in range(1, 8)]
    for target in targets:
        pl.semaphore_signal(barrier, inc=1, device_id=target, device_id_type=MESH)
    pl.semaphore_wait(barrier, len(targets))


class Links:
    def __init__(self, send, recv):
        self.send, self.recv, self.used, self.sent = send, recv, 0, []

    def to(self, src, dst, target):
        copy = pltpu.make_async_remote_copy(
            src_ref=src,
            dst_ref=dst,
            send_sem=self.send.at[self.used],
            recv_sem=self.recv.at[self.used],
            device_id=target,
            device_id_type=MESH,
        )
        self.used += 1
        copy.start()
        self.sent.append(copy)
        return copy

    def finish(self):
        for copy in self.sent:
            copy.wait_send()


class Gather:
    def __init__(self, me, links, own, slot):
        self.me, self.links, self.slot = me, links, slot
        here = slot(me.x, me.c)
        self.a = links.to(own, here, {"tensor_0": me.xp})
        self.b = links.to(own, here, {"tensor_0": me.xm})
        self.s0 = links.to(own, here, {"tensor_1": me.sib})

    def first(self):
        me = self.me
        self.a.wait_recv()
        block = self.slot(me.xm, me.c)
        self.f = self.links.to(block, block, {"tensor_0": me.xp})
        self.s1 = self.links.to(block, block, {"tensor_1": me.sib})

    def second(self):
        me = self.me
        self.b.wait_recv()
        block = self.slot(me.xp, me.c)
        self.s2 = self.links.to(block, block, {"tensor_1": me.sib})

    def third(self):
        me = self.me
        self.f.wait_recv()
        block = self.slot(me.xo, me.c)
        self.s3 = self.links.to(block, block, {"tensor_1": me.sib})

    def rest(self):
        for copy in (self.s0, self.s1, self.s2, self.s3):
            copy.wait_recv()


class RingSum:
    def __init__(self, links, axis, places, src, came, stage):
        own, plus, minus, far = places
        self.links, self.axis, self.src = links, axis, src
        self.own, self.plus, self.came, self.stage = own, plus, came, stage
        self.far = links.to(src(far), came.at[0], {axis: plus})
        self.near = links.to(src(minus), came.at[1], {axis: minus})

    def middle(self):
        self.far.wait_recv()
        self.stage[...] = self.came[0] + self.src(self.plus)[...]
        self.last = self.links.to(self.stage, self.came.at[2], {self.axis: self.plus})

    def total(self):
        self.near.wait_recv()
        self.last.wait_recv()
        return self.src(self.own)[...] + self.came[1] + self.came[2]


class RingSpread:
    def __init__(self, links, axis, places, slot):
        own, plus, minus, _ = places
        self.links, self.axis, self.plus = links, axis, plus
        self.from_minus = slot(minus)
        self.up = links.to(slot(own), slot(own), {axis: plus})
        self.down = links.to(slot(own), slot(own), {axis: minus})

    def middle(self):
        self.up.wait_recv()
        self.far = self.links.to(self.from_minus, self.from_minus, {self.axis: self.plus})

    def finish(self):
        self.down.wait_recv()
        self.far.wait_recv()


def three(a, b, dims=((1,), (0,))):
    dot = lambda p, q: lax.dot_general(p, q, (dims, ((), ())), preferred_element_type=F32)
    return dot(a[0], b[0]) + dot(a[0], b[1]) + dot(a[1], b[0])


def rows_at(start, size, unit=8):
    return pl.ds(pl.multiple_of(start, unit), size)


def eliminate(d):
    lane = lax.broadcasted_iota(jnp.int32, (64, 128), 1)
    row = lax.broadcasted_iota(jnp.int32, (64, 128), 0)
    e = jnp.where(lane < 64, d, jnp.where(lane - 64 == row, 1.0, 0.0).astype(F32))

    def panel(p, e):
        live = 64 - 8 * p
        for first in range(0, 8, 8):
            cols = [jnp.broadcast_to(e[:, j : j + 1], (64, 128)) for j in range(first, first + 8)]
            for n, col in enumerate(cols):
                j = first + n
                weight = pltpu.reciprocal(col[j : j + 1])
                factor = jnp.where((row > j) & (row < live), col, 0.0) * weight
                e = e - factor * e[j : j + 1]
                for m in range(n + 1, 8):
                    cols[m] = cols[m] - factor * col[first + m : first + m + 1]
        e = pltpu.roll(e, 120, 1)
        return jnp.concatenate([e[8:], e[:8]], axis=0)

    e = lax.fori_loop(0, 8, panel, e)
    v = e[:, :64]
    diag = jnp.sum(jnp.where(lane - 64 == row, e, 0.0), axis=1, keepdims=True)
    return v * lax.rsqrt(diag)


def exact(a, b, dims=((1,), (0,))):
    return lax.dot_general(a, b, (dims, ((), ())), precision=HIGH, preferred_element_type=F32)


def factor_block(k, a, inv):
    rows = slice(64 * k, 64 * k + 64)
    block = a[rows, 128 * (k // 2) : 128 * (k // 2) + 128]
    if k % 2:
        block = pltpu.roll(block, 64, 1)
    v = eliminate(block)
    inv_row = exact(v, inv[rows, :])
    inv[rows, :] = inv_row
    if k < 3:
        u = exact(v, a[rows, :])
        below = u.T[64 * (k + 1) :, :]
        rest = slice(64 * (k + 1), 256)
        a[rest, :] = a[rest, :] - exact(below, u)
        inv[rest, :] = inv[rest, :] - exact(below, inv_row)


def step_kernel(
    acts, og, mom, q, buf_out, ob, wide_out, ortho_out, q_out,
    actsv, acts_t, buf, qg, qh, ql, yg, yh, yl, ogg, y_own,
    part, r_left, s1, chunk, zr, zs, full,
    bth, btl, lh, ll, gram, gram_r, gram_s, a, inv,
    cc, c_sib, c_sum, rx, sx, tx, ry, sy, ty, rxy, sxy, ryx, syx,
    rest, zr2, zs2, all_z, own_right, wide, sq,
    send, recv, local,
):
    me = Place()
    links = Links(send, recv)
    own_q = qg.at[me.x * 2 + me.c]
    own_rows = pl.ds(pl.multiple_of(me.c * 128, 128), 128)
    own_og = ogg.at[me.x, own_rows]
    loads = [
        pltpu.make_async_copy(q, own_q, local.at[0]),
        pltpu.make_async_copy(og, own_og, local.at[1]),
        pltpu.make_async_copy(acts, actsv, local.at[2]),
        pltpu.make_async_copy(mom, buf, local.at[3]),
    ]
    for load in loads:
        load.start()
    greet(me)
    gq = Gather(me, links, q, lambda x, c: qg.at[x * 2 + c])
    gq.first()
    gq.second()
    loads[2].wait()
    for j in range(4):
        acts_t[j] = actsv[256 * j : 256 * (j + 1), :].T
    loads[0].wait()
    loads[1].wait()
    loads[3].wait()
    own = ogg.at[me.x, own_rows]

    def take(x, c, first=False):
        b = 2 * x + c
        rows = rows_at(b * 256, 256, 256)
        high, low = halves(qg[b])
        qh[rows, :], ql[rows, :] = high, low
        lhs = own[:, rows]
        share = mxu(lhs, high) + mxu(lhs, low)
        y_own[...] = share if first else y_own[...] + share

    take(me.x, me.c, True)
    take(me.xm, me.c)
    take(me.xp, me.c)
    gq.s0.wait_recv()
    take(me.x, me.sib)
    gq.third()
    take(me.xo, me.c)
    gq.s1.wait_recv()
    take(me.xp, me.sib)
    gq.s2.wait_recv()
    take(me.xm, me.sib)
    gq.s3.wait_recv()
    take(me.xo, me.sib)
    yg[me.x, own_rows, :] = y_own[...]
    own_y = yg.at[me.x, own_rows]
    gy = Gather(me, links, own_y, lambda x, c: yg.at[x, pl.ds(pl.multiple_of(c * 128, 128), 128)])

    def momentum_part(t):
        rows = rows_at(t * 128, 128)
        share = three(halves(buf[rows, :]), (qh[...], ql[...]))
        for half in range(2):
            part[half, rows, :] = share[:, 128 * half : 128 * half + 128]

    pl.loop(0, 3)(momentum_part)
    gy.first()
    gy.second()
    pl.loop(3, 5)(momentum_part)
    gy.third()
    gy.rest()
    go = Gather(
        me, links, og, lambda x, c: ogg.at[x, pl.ds(pl.multiple_of(c * 128, 128), 128)]
    )
    for j in range(4):
        high, low = halves(yg[j])
        yh[j], yl[j] = high, low

    @pl.loop(0, 5)
    def _(t):
        rows = pl.ds(pl.multiple_of(t * 128, 128), 128)
        acc = jnp.zeros((128, 256), F32)
        for j in range(4):
            lhs = acts_t[j, rows, :]
            acc += mxu(lhs, yh[j]) + mxu(lhs, yl[j])
        for half in range(2):
            piece = acc[:, 128 * half : 128 * half + 128]
            part[half, rows, :] = (0.95 * part[half, rows, :] + piece) * (1 / 32)

    def of_y(ref, y):
        return ref.at[:, pl.ds(pl.multiple_of(y * 160, 32), 160)]

    ys, xs = (me.y, me.yp, me.ym, me.yo), (me.x, me.xp, me.xm, me.xo)
    ring = RingSum(links, "dp_0", ys, lambda y: of_y(part, y), r_left, s1)
    ring.middle()
    chunk[...] = ring.total()

    def z_rows(z):
        return z // 4, pl.multiple_of(lax.rem(z, 4) * 40, 8)

    came = []
    for k in range(1, 8):
        half, row = z_rows(me.zk(k))
        came.append(
            links.to(chunk.at[half, pl.ds(row, 40)], zr.at[k - 1], {"dp_1": me.zk(k)})
        )
    go.first()
    go.second()
    half, row = z_rows(me.z)
    for copy in came:
        copy.wait_recv()
    total = chunk[half, pl.ds(row, 40), :]
    for k in range(7):
        total += zr[k]
    zs[...] = total
    spot = full.at[half, pl.ds(pl.multiple_of(me.y * 160 + row, 8), 40)]
    came = [links.to(zs, spot, {"dp_1": me.zk(k)}) for k in range(1, 8)]
    spot[...] = total
    go.third()
    for copy in came:
        copy.wait_recv()
    spread = RingSpread(links, "dp_0", ys, lambda y: of_y(full, y))

    def buffer_part(n):
        cols = rows_at(n * 256, 256, 256)
        acc = 0.95 * buf[:, cols]
        for j in range(4):
            acc += mxu(acts_t[j], ogg[j, :, cols])
        buf[:, cols] = acc
        bth[cols, :], btl[cols, :] = halves(acc.T)

    go.rest()
    pl.loop(0, 4)(buffer_part)
    spread.middle()
    pl.loop(4, 8)(buffer_part)
    store = pltpu.make_async_copy(buf, buf_out, local.at[4])
    store.start()
    spread.finish()
    lt = []
    for half in range(2):
        cols = slice(128 * half, 128 * half + 128)
        lh[:, cols], ll[:, cols] = halves(full[half])
        lt.append(full[half].T)
    left = lh[...], ll[...]
    gram[...] = three(halves(jnp.concatenate(lt, axis=0)), left)

    def product_with(core):
        @pl.loop(0, 4)
        def _(n):
            rows = rows_at((2 * n + core) * 256, 256, 256)
            cc[n, core] = three((bth[rows, :], btl[rows, :]), (lh[...], ll[...]))

    index = 2 * me.x + me.c
    gram_in = []
    for peer, there in me.tensor_peers():
        gram_in.append(links.to(gram.at[rows_at(there * 32, 32)], gram_r.at[index], peer))
    gram_r[index] = gram[rows_at(index * 32, 32), :]
    product_with(me.sib)
    swap = links.to(cc.at[:, me.sib], c_sib, {"tensor_1": me.sib})
    for copy in gram_in:
        copy.wait_recv()
    total = gram_r[0]
    for b in range(1, 8):
        total += gram_r[b]
    gram_s[...] = total
    gram_rows = a.at[rows_at(index * 32, 32)]
    gram_in = [links.to(gram_s, gram_rows, peer) for peer, _ in me.tensor_peers()]
    gram_rows[...] = total
    product_with(me.c)
    swap.wait_recv()
    c_sum[...] = cc[:, me.c].reshape(4, 2, 128, 256) + c_sib[...].reshape(4, 2, 128, 256)
    x_first = RingSum(links, "tensor_0", xs, lambda x: c_sum.at[x, 0], rx, sx)
    y_first = RingSum(
        links, "dp_0", ys, lambda y: c_sum.at[:, 1, rows_at(y * 32, 32)], ry, sy
    )
    same = lax.broadcasted_iota(jnp.int32, (256, 256), 0) == lax.broadcasted_iota(
        jnp.int32, (256, 256), 1
    )
    inv[...] = jnp.where(same, 1.0, 0.0).astype(F32)
    y_first.middle()
    x_first.middle()
    for copy in gram_in:
        copy.wait_recv()

    factor_block(0, a, inv)
    tx[...] = x_first.total()
    then_y = RingSum(links, "dp_0", ys, lambda y: tx.at[rows_at(y * 32, 32)], ryx, syx)
    ty[...] = y_first.total()
    then_x = RingSum(links, "tensor_0", xs, lambda x: ty.at[x], rxy, sxy)
    factor_block(1, a, inv)
    then_y.middle()
    then_x.middle()
    factor_block(2, a, inv)
    rest[:32, :] = then_y.total()
    rest[32:, :] = then_x.total()
    came = [
        links.to(rest.at[rows_at(me.zk(k) * 8, 8)], zr2.at[k - 1], {"dp_1": me.zk(k)})
        for k in range(1, 8)
    ]
    factor_block(3, a, inv)
    for copy in came:
        copy.wait_recv()
    total = rest[rows_at(me.z * 8, 8), :]
    for k in range(7):
        total += zr2[k]
    total = total * (1 / 32)
    zs2[...] = total
    spot = all_z.at[rows_at(me.z * 8, 8)]
    came = [links.to(zs2, spot, {"dp_1": me.zk(k)}) for k in range(1, 8)]
    spot[...] = total
    inverse = halves(inv[...])
    across = ((1,), (1,))
    for copy in came:
        copy.wait_recv()
    mine = three(halves(all_z[...]), inverse, across)
    own_right[0, rows_at(me.y * 32, 32), :] = mine[:32]
    own_right[1, rows_at(me.y * 32, 32), :] = mine[32:]
    right_y = RingSpread(
        links, "dp_0", ys, lambda y: own_right.at[:, rows_at(y * 32, 32)]
    )
    ortho = three((lh[...], ll[...]), inverse, across)
    ortho_out[...] = ortho
    ob[...] = (ortho * 0.05).astype(BF16)
    right_y.middle()
    right_y.finish()
    wide[index, :128, :] = own_right[0].astype(BF16)
    wide[index, 128:, :] = own_right[1].astype(BF16)
    gw = Gather(me, links, wide.at[index], lambda x, c: wide.at[2 * x + c])
    values = own_right[...].reshape(256, 256)
    sq[index] = jnp.broadcast_to(jnp.sum(values * values, axis=0, keepdims=True), (8, 256))
    mark = sq.at[index]
    came = [links.to(mark, mark, peer) for peer, _ in me.tensor_peers()]
    gw.first()
    gw.second()
    for copy in came:
        copy.wait_recv()
    squares = sq[0]
    for b in range(1, 8):
        squares += sq[b]
    q_out[...] = values * lax.rsqrt(squares[:1] + 1e-06)
    gw.third()
    gw.rest()
    wide_out[...] = wide[...]
    store.wait()
    links.finish()


def apply_kernel(buf, ob, wide, ortho, q, new_out, ortho_out, q_out):
    lhs = ob[...]
    for b in range(8):
        cols = slice(256 * b, 256 * b + 256)
        update = lax.dot_general(
            lhs, wide[b], (((1,), (1,)), ((), ())), preferred_element_type=F32
        )
        new_out[:, cols] = buf[:, cols] - update
    ortho_out[...] = ortho[...]
    q_out[...] = q[...]


def apply_update(buf, ob, wide, ortho, q):
    def tile(rows, cols):
        return pl.BlockSpec((rows, cols), lambda i: (i, 0))

    return pl.pallas_call(
        apply_kernel,
        grid=(8,),
        out_shape=(
            jax.ShapeDtypeStruct((640, 2048), F32),
            jax.ShapeDtypeStruct((640, 256), F32),
            jax.ShapeDtypeStruct((256, 256), F32),
        ),
        in_specs=[
            tile(80, 2048),
            tile(80, 256),
            pl.BlockSpec((8, 256, 256), lambda i: (0, 0, 0)),
            tile(80, 256),
            tile(32, 256),
        ],
        out_specs=(tile(80, 2048), tile(80, 256), tile(32, 256)),
        compiler_params=pltpu.CompilerParams(vmem_limit_bytes=56 * 2**20),
        name="apply_update",
    )(buf, ob, wide, ortho, q)


def whole_step(acts, out_grad, momentum, q_basis):
    any_space = pl.BlockSpec(memory_space=pl.ANY)
    in_hbm = pl.BlockSpec(memory_space=pltpu.HBM)
    in_vmem = pl.BlockSpec(memory_space=pltpu.VMEM)
    copies = 120
    vm = pltpu.VMEM
    scratch = [
        vm((1024, 640), BF16),
        vm((4, 640, 256), BF16),
        vm((640, 2048), F32),
        vm((8, 256, 256), F32),
        vm((2048, 256), BF16),
        vm((2048, 256), BF16),
        vm((4, 256, 256), F32),
        vm((4, 256, 256), BF16),
        vm((4, 256, 256), BF16),
        vm((4, 256, 2048), BF16),
        vm((128, 256), F32),
        vm((2, 640, 128), F32),
        vm((3, 2, 160, 128), F32),
        vm((2, 160, 128), F32),
        vm((2, 160, 128), F32),
        vm((7, 40, 128), F32),
        vm((40, 128), F32),
        vm((2, 640, 128), F32),
        vm((2048, 640), BF16),
        vm((2048, 640), BF16),
        vm((640, 256), BF16),
        vm((640, 256), BF16),
        vm((256, 256), F32),
        vm((8, 32, 256), F32),
        vm((32, 256), F32),
        vm((256, 256), F32),
        vm((256, 256), F32),
        vm((4, 2, 256, 256), F32),
        vm((4, 256, 256), F32),
        vm((4, 2, 128, 256), F32),
        vm((3, 128, 256), F32),
        vm((128, 256), F32),
        vm((128, 256), F32),
        vm((3, 4, 32, 256), F32),
        vm((4, 32, 256), F32),
        vm((4, 32, 256), F32),
        vm((3, 32, 256), F32),
        vm((32, 256), F32),
        vm((3, 32, 256), F32),
        vm((32, 256), F32),
        vm((64, 256), F32),
        vm((7, 8, 256), F32),
        vm((8, 256), F32),
        vm((64, 256), F32),
        vm((2, 128, 256), F32),
        vm((8, 256, 256), BF16),
        vm((8, 8, 256), F32),
        pltpu.SemaphoreType.DMA((copies,)),
        pltpu.SemaphoreType.DMA((copies,)),
        pltpu.SemaphoreType.DMA((12,)),
    ]
    outs = pl.pallas_call(
        step_kernel,
        out_shape=(
            jax.ShapeDtypeStruct((640, 2048), F32),
            jax.ShapeDtypeStruct((640, 256), BF16),
            jax.ShapeDtypeStruct((8, 256, 256), BF16),
            jax.ShapeDtypeStruct((640, 256), F32),
            jax.ShapeDtypeStruct((256, 256), F32),
        ),
        in_specs=[in_hbm] * 4,
        out_specs=(any_space, in_vmem, in_vmem, in_vmem, in_vmem),
        scratch_shapes=scratch,
        compiler_params=pltpu.CompilerParams(
            collective_id=0, has_side_effects=True, vmem_limit_bytes=60 * 2**20
        ),
        name="whole_step",
    )(acts, out_grad, momentum, q_basis)
    return apply_update(*outs)


def solution(mesh):
    split = Mesh(mesh.devices.reshape(4, 8, 4, 2), ("dp_0", "dp_1", "tensor_0", "tensor_1"))
    return jax.shard_map(
        whole_step,
        mesh=split,
        in_specs=(P(DP, TENSOR), P(DP_TENSOR, None), P(DP_TENSOR, None), P(TENSOR, None)),
        out_specs=(P(DP_TENSOR, None), P(TENSOR, None), P(TENSOR, None)),
        check_vma=False,
    )
```

```python
import jax
import jax.numpy as jnp
from jax import lax
from jax.experimental import pallas as pl
from jax.experimental.pallas import tpu as pltpu
from jax.sharding import Mesh
from jax.sharding import PartitionSpec as P

DP = ("dp_0", "dp_1")
TENSOR = ("tensor_0", "tensor_1")
DP_TENSOR = ("dp_0", "dp_1", "tensor_0", "tensor_1")
HIGH = lax.Precision.HIGHEST
F32, BF16 = jnp.float32, jnp.bfloat16
MESH = pl.DeviceIdType.MESH


def halves(value):
    high = value.astype(BF16)
    return high, (value - high.astype(F32)).astype(BF16)


def mxu(a, b):
    return lax.dot_general(a, b, (((1,), (0,)), ((), ())), preferred_element_type=F32)


class Place:
    def __init__(self):
        self.y, self.z = lax.axis_index("dp_0"), lax.axis_index("dp_1")
        self.x, self.c = lax.axis_index("tensor_0"), lax.axis_index("tensor_1")
        step = 1 - 2 * self.c
        self.sib = 1 - self.c
        self.xp, self.xm = lax.rem(self.x + step + 4, 4), lax.rem(self.x - step + 4, 4)
        self.yp, self.ym = lax.rem(self.y + step + 4, 4), lax.rem(self.y - step + 4, 4)
        self.xo, self.yo = lax.rem(self.x + 2, 4), lax.rem(self.y + 2, 4)

    def tensor_peers(self):
        peers = [({"tensor_1": self.sib}, 2 * self.x + self.sib)]
        for n in range(1, 4):
            there = lax.rem(self.x + n, 4)
            for core in (self.c, self.sib):
                peers.append(({"tensor_0": there, "tensor_1": core}, 2 * there + core))
        return peers

    def zk(self, k):
        return lax.rem(self.z + k, 8)


def greet(me):
    barrier = pltpu.get_barrier_semaphore()
    targets = [peer for peer, _ in me.tensor_peers()]
    targets += [{"dp_0": me.yp}, {"dp_0": me.ym}, {"dp_0": me.yo}]
    targets += [{"dp_1": me.zk(k)} for k in range(1, 8)]
    for target in targets:
        pl.semaphore_signal(barrier, inc=1, device_id=target, device_id_type=MESH)
    pl.semaphore_wait(barrier, len(targets))


class Links:
    def __init__(self, send, recv):
        self.send, self.recv, self.used, self.sent = send, recv, 0, []

    def to(self, src, dst, target):
        copy = pltpu.make_async_remote_copy(
            src_ref=src,
            dst_ref=dst,
            send_sem=self.send.at[self.used],
            recv_sem=self.recv.at[self.used],
            device_id=target,
            device_id_type=MESH,
        )
        self.used += 1
        copy.start()
        self.sent.append(copy)
        return copy

    def finish(self):
        for copy in self.sent:
            copy.wait_send()


class Gather:
    def __init__(self, me, links, own, slot):
        self.me, self.links, self.slot = me, links, slot
        here = slot(me.x, me.c)
        self.a = links.to(own, here, {"tensor_0": me.xp})
        self.b = links.to(own, here, {"tensor_0": me.xm})
        self.s0 = links.to(own, here, {"tensor_1": me.sib})

    def first(self):
        me = self.me
        self.a.wait_recv()
        block = self.slot(me.xm, me.c)
        self.f = self.links.to(block, block, {"tensor_0": me.xp})
        self.s1 = self.links.to(block, block, {"tensor_1": me.sib})

    def second(self):
        me = self.me
        self.b.wait_recv()
        block = self.slot(me.xp, me.c)
        self.s2 = self.links.to(block, block, {"tensor_1": me.sib})

    def third(self):
        me = self.me
        self.f.wait_recv()
        block = self.slot(me.xo, me.c)
        self.s3 = self.links.to(block, block, {"tensor_1": me.sib})

    def rest(self):
        for copy in (self.s0, self.s1, self.s2, self.s3):
            copy.wait_recv()


class RingSum:
    def __init__(self, links, axis, places, src, came, stage):
        own, plus, minus, far = places
        self.links, self.axis, self.src = links, axis, src
        self.own, self.plus, self.came, self.stage = own, plus, came, stage
        self.far = links.to(src(far), came.at[0], {axis: plus})
        self.near = links.to(src(minus), came.at[1], {axis: minus})

    def middle(self):
        self.far.wait_recv()
        self.stage[...] = self.came[0] + self.src(self.plus)[...]
        self.last = self.links.to(self.stage, self.came.at[2], {self.axis: self.plus})

    def total(self):
        self.near.wait_recv()
        self.last.wait_recv()
        return self.src(self.own)[...] + self.came[1] + self.came[2]


class RingSpread:
    def __init__(self, links, axis, places, slot):
        own, plus, minus, _ = places
        self.links, self.axis, self.plus = links, axis, plus
        self.from_minus = slot(minus)
        self.up = links.to(slot(own), slot(own), {axis: plus})
        self.down = links.to(slot(own), slot(own), {axis: minus})

    def middle(self):
        self.up.wait_recv()
        self.far = self.links.to(self.from_minus, self.from_minus, {self.axis: self.plus})

    def finish(self):
        self.down.wait_recv()
        self.far.wait_recv()


class DirectSum:
    def __init__(self, links, axis, places, src, came):
        own, *others = places
        self.mine, self.came = src(own), came
        self.copies = [
            links.to(src(there), came.at[n], {axis: there}) for n, there in enumerate(others)
        ]

    def total(self):
        for copy in self.copies:
            copy.wait_recv()
        return self.mine[...] + self.came[0] + self.came[1] + self.came[2]


def three(a, b, dims=((1,), (0,))):
    dot = lambda p, q: lax.dot_general(p, q, (dims, ((), ())), preferred_element_type=F32)
    return dot(a[0], b[0]) + dot(a[0], b[1]) + dot(a[1], b[0])


def rows_at(start, size, unit=8):
    return pl.ds(pl.multiple_of(start, unit), size)


def eliminate(d):
    lane = lax.broadcasted_iota(jnp.int32, (64, 128), 1)
    row = lax.broadcasted_iota(jnp.int32, (64, 128), 0)
    e = jnp.where(lane < 64, d, jnp.where(lane - 64 == row, 1.0, 0.0).astype(F32))

    def panel(p, e):
        live = 64 - 8 * p
        for first in range(0, 8, 8):
            cols = [jnp.broadcast_to(e[:, j : j + 1], (64, 128)) for j in range(first, first + 8)]
            for n, col in enumerate(cols):
                j = first + n
                weight = pltpu.reciprocal(col[j : j + 1])
                factor = jnp.where((row > j) & (row < live), col, 0.0) * weight
                e = e - factor * e[j : j + 1]
                for m in range(n + 1, 8):
                    cols[m] = cols[m] - factor * col[first + m : first + m + 1]
        e = pltpu.roll(e, 120, 1)
        return jnp.concatenate([e[8:], e[:8]], axis=0)

    e = lax.fori_loop(0, 8, panel, e)
    v = e[:, :64]
    diag = jnp.sum(jnp.where(lane - 64 == row, e, 0.0), axis=1, keepdims=True)
    return v * lax.rsqrt(diag)


def exact(a, b, dims=((1,), (0,))):
    return lax.dot_general(a, b, (dims, ((), ())), precision=HIGH, preferred_element_type=F32)


def factor_block(k, a, inv):
    rows = slice(64 * k, 64 * k + 64)
    block = a[rows, 128 * (k // 2) : 128 * (k // 2) + 128]
    if k % 2:
        block = pltpu.roll(block, 64, 1)
    v = eliminate(block)
    inv_row = exact(v, inv[rows, :])
    inv[rows, :] = inv_row
    if k < 3:
        u = exact(v, a[rows, :])
        below = u.T[64 * (k + 1) :, :]
        rest = slice(64 * (k + 1), 256)
        a[rest, :] = a[rest, :] - exact(below, u)
        inv[rest, :] = inv[rest, :] - exact(below, inv_row)


def step_kernel(
    acts, og, mom, q, buf_out, ob, wide_out, ortho_out, q_out,
    actsv, acts_t, buf, qg, qh, ql, yg, yh, yl, ogg, y_own,
    part, r_left, s1, chunk, zr, zs, full,
    bth, btl, lh, ll, gram, gram_r, gram_s, a, inv,
    cc, c_sib, c_sum, rx, sx, tx, ry, sy, ty, rxy, ryx,
    rest, zr2, zs2, all_z, own_right, wide, sq,
    send, recv, local,
):
    me = Place()
    links = Links(send, recv)
    own_q = qg.at[me.x * 2 + me.c]
    own_rows = pl.ds(pl.multiple_of(me.c * 128, 128), 128)
    own_og = ogg.at[me.x, own_rows]
    loads = [
        pltpu.make_async_copy(q, own_q, local.at[0]),
        pltpu.make_async_copy(og, own_og, local.at[1]),
        pltpu.make_async_copy(acts, actsv, local.at[2]),
        pltpu.make_async_copy(mom, buf, local.at[3]),
    ]
    for load in loads:
        load.start()
    greet(me)
    gq = Gather(me, links, q, lambda x, c: qg.at[x * 2 + c])
    gq.first()
    gq.second()
    loads[2].wait()
    for j in range(4):
        acts_t[j] = actsv[256 * j : 256 * (j + 1), :].T
    loads[0].wait()
    loads[1].wait()
    loads[3].wait()
    own = ogg.at[me.x, own_rows]

    def take(x, c, first=False):
        b = 2 * x + c
        rows = rows_at(b * 256, 256, 256)
        high, low = halves(qg[b])
        qh[rows, :], ql[rows, :] = high, low
        lhs = own[:, rows]
        share = mxu(lhs, high) + mxu(lhs, low)
        y_own[...] = share if first else y_own[...] + share

    take(me.x, me.c, True)
    take(me.xm, me.c)
    take(me.xp, me.c)
    gq.s0.wait_recv()
    take(me.x, me.sib)
    gq.third()
    take(me.xo, me.c)
    gq.s1.wait_recv()
    take(me.xp, me.sib)
    gq.s2.wait_recv()
    take(me.xm, me.sib)
    gq.s3.wait_recv()
    take(me.xo, me.sib)
    yg[me.x, own_rows, :] = y_own[...]
    own_y = yg.at[me.x, own_rows]
    gy = Gather(me, links, own_y, lambda x, c: yg.at[x, pl.ds(pl.multiple_of(c * 128, 128), 128)])

    def momentum_part(t):
        rows = rows_at(t * 128, 128)
        share = three(halves(buf[rows, :]), (qh[...], ql[...]))
        for half in range(2):
            part[half, rows, :] = share[:, 128 * half : 128 * half + 128]

    pl.loop(0, 3)(momentum_part)
    gy.first()
    gy.second()
    pl.loop(3, 5)(momentum_part)
    gy.third()
    gy.rest()
    go = Gather(
        me, links, og, lambda x, c: ogg.at[x, pl.ds(pl.multiple_of(c * 128, 128), 128)]
    )
    for j in range(4):
        high, low = halves(yg[j])
        yh[j], yl[j] = high, low

    @pl.loop(0, 5)
    def _(t):
        rows = pl.ds(pl.multiple_of(t * 128, 128), 128)
        acc = jnp.zeros((128, 256), F32)
        for j in range(4):
            lhs = acts_t[j, rows, :]
            acc += mxu(lhs, yh[j]) + mxu(lhs, yl[j])
        for half in range(2):
            piece = acc[:, 128 * half : 128 * half + 128]
            part[half, rows, :] = (0.95 * part[half, rows, :] + piece) * (1 / 32)

    def of_y(ref, y):
        return ref.at[:, pl.ds(pl.multiple_of(y * 160, 32), 160)]

    ys, xs = (me.y, me.yp, me.ym, me.yo), (me.x, me.xp, me.xm, me.xo)
    ring = RingSum(links, "dp_0", ys, lambda y: of_y(part, y), r_left, s1)
    ring.middle()
    chunk[...] = ring.total()

    def z_rows(z):
        return z // 4, pl.multiple_of(lax.rem(z, 4) * 40, 8)

    came = []
    for k in range(1, 8):
        half, row = z_rows(me.zk(k))
        came.append(
            links.to(chunk.at[half, pl.ds(row, 40)], zr.at[k - 1], {"dp_1": me.zk(k)})
        )
    go.first()
    go.second()
    half, row = z_rows(me.z)
    for copy in came:
        copy.wait_recv()
    total = chunk[half, pl.ds(row, 40), :]
    for k in range(7):
        total += zr[k]
    zs[...] = total
    spot = full.at[half, pl.ds(pl.multiple_of(me.y * 160 + row, 8), 40)]
    came = [links.to(zs, spot, {"dp_1": me.zk(k)}) for k in range(1, 8)]
    spot[...] = total
    go.third()
    for copy in came:
        copy.wait_recv()
    spread = RingSpread(links, "dp_0", ys, lambda y: of_y(full, y))

    def buffer_part(n):
        cols = rows_at(n * 256, 256, 256)
        acc = 0.95 * buf[:, cols]
        for j in range(4):
            acc += mxu(acts_t[j], ogg[j, :, cols])
        buf[:, cols] = acc
        bth[cols, :], btl[cols, :] = halves(acc.T)

    go.rest()
    pl.loop(0, 4)(buffer_part)
    spread.middle()
    pl.loop(4, 8)(buffer_part)
    store = pltpu.make_async_copy(buf, buf_out, local.at[4])
    store.start()
    spread.finish()
    lt = []
    for half in range(2):
        cols = slice(128 * half, 128 * half + 128)
        lh[:, cols], ll[:, cols] = halves(full[half])
        lt.append(full[half].T)
    left = lh[...], ll[...]
    gram[...] = three(halves(jnp.concatenate(lt, axis=0)), left)

    def product_with(core):
        @pl.loop(0, 4)
        def _(n):
            rows = rows_at((2 * n + core) * 256, 256, 256)
            cc[n, core] = three((bth[rows, :], btl[rows, :]), (lh[...], ll[...]))

    index = 2 * me.x + me.c
    gram_in = []
    for peer, there in me.tensor_peers():
        gram_in.append(links.to(gram.at[rows_at(there * 32, 32)], gram_r.at[index], peer))
    gram_r[index] = gram[rows_at(index * 32, 32), :]
    product_with(me.sib)
    swap = links.to(cc.at[:, me.sib], c_sib, {"tensor_1": me.sib})
    for copy in gram_in:
        copy.wait_recv()
    total = gram_r[0]
    for b in range(1, 8):
        total += gram_r[b]
    gram_s[...] = total
    gram_rows = a.at[rows_at(index * 32, 32)]
    gram_in = [links.to(gram_s, gram_rows, peer) for peer, _ in me.tensor_peers()]
    gram_rows[...] = total
    product_with(me.c)
    swap.wait_recv()
    c_sum[...] = cc[:, me.c].reshape(4, 2, 128, 256) + c_sib[...].reshape(4, 2, 128, 256)
    x_first = RingSum(links, "tensor_0", xs, lambda x: c_sum.at[x, 0], rx, sx)
    y_first = RingSum(
        links, "dp_0", ys, lambda y: c_sum.at[:, 1, rows_at(y * 32, 32)], ry, sy
    )
    same = lax.broadcasted_iota(jnp.int32, (256, 256), 0) == lax.broadcasted_iota(
        jnp.int32, (256, 256), 1
    )
    inv[...] = jnp.where(same, 1.0, 0.0).astype(F32)
    for copy in gram_in:
        copy.wait_recv()
    factor_block(0, a, inv)
    y_first.middle()
    x_first.middle()
    factor_block(1, a, inv)
    tx[...] = x_first.total()
    then_y = DirectSum(links, "dp_0", ys, lambda y: tx.at[rows_at(y * 32, 32)], ryx)
    ty[...] = y_first.total()
    then_x = DirectSum(links, "tensor_0", xs, lambda x: ty.at[x], rxy)
    factor_block(2, a, inv)
    rest[:32, :] = then_y.total()
    rest[32:, :] = then_x.total()
    came = [
        links.to(rest.at[rows_at(me.zk(k) * 8, 8)], zr2.at[k - 1], {"dp_1": me.zk(k)})
        for k in range(1, 8)
    ]
    factor_block(3, a, inv)
    for copy in came:
        copy.wait_recv()
    total = rest[rows_at(me.z * 8, 8), :]
    for k in range(7):
        total += zr2[k]
    total = total * (1 / 32)
    zs2[...] = total
    spot = all_z.at[rows_at(me.z * 8, 8)]
    came = [links.to(zs2, spot, {"dp_1": me.zk(k)}) for k in range(1, 8)]
    spot[...] = total
    inverse = halves(inv[...])
    across = ((1,), (1,))
    for copy in came:
        copy.wait_recv()
    mine = three(halves(all_z[...]), inverse, across)
    own_right[0, rows_at(me.y * 32, 32), :] = mine[:32]
    own_right[1, rows_at(me.y * 32, 32), :] = mine[32:]
    own_part = own_right.at[:, rows_at(me.y * 32, 32)]
    came = [links.to(own_part, own_part, {"dp_0": there}) for there in ys[1:]]
    ortho = three((lh[...], ll[...]), inverse, across)
    ortho_out[...] = ortho
    ob[...] = (ortho * 0.05).astype(BF16)
    for copy in came:
        copy.wait_recv()
    wide[index, :128, :] = own_right[0].astype(BF16)
    wide[index, 128:, :] = own_right[1].astype(BF16)
    gw = Gather(me, links, wide.at[index], lambda x, c: wide.at[2 * x + c])
    values = own_right[...].reshape(256, 256)
    sq[index] = jnp.broadcast_to(jnp.sum(values * values, axis=0, keepdims=True), (8, 256))
    mark = sq.at[index]
    came = [links.to(mark, mark, peer) for peer, _ in me.tensor_peers()]
    gw.first()
    gw.second()
    for copy in came:
        copy.wait_recv()
    squares = sq[0]
    for b in range(1, 8):
        squares += sq[b]
    q_out[...] = values * lax.rsqrt(squares[:1] + 1e-06)
    gw.third()
    gw.rest()
    wide_out[...] = wide[...]
    store.wait()
    links.finish()


def apply_kernel(buf, ob, wide, ortho, q, new_out, ortho_out, q_out):
    for b in range(2):
        cols = slice(256 * b, 256 * b + 256)
        update = lax.dot_general(
            ob[...], wide[b], (((1,), (1,)), ((), ())), preferred_element_type=F32
        )
        new_out[:, cols] = buf[:, cols] - update
    ortho_out[...] = ortho[...]
    q_out[...] = q[...]


def apply_update(buf, ob, wide, ortho, q):
    def rows(height):
        return pl.BlockSpec((height, 256), lambda i: (i, 0))

    cols = pl.BlockSpec((640, 512), lambda i: (0, i))
    return pl.pallas_call(
        apply_kernel,
        grid=(4,),
        out_shape=(
            jax.ShapeDtypeStruct((640, 2048), F32),
            jax.ShapeDtypeStruct((640, 256), F32),
            jax.ShapeDtypeStruct((256, 256), F32),
        ),
        in_specs=[
            cols,
            pl.BlockSpec((640, 256), lambda i: (0, 0)),
            pl.BlockSpec((2, 256, 256), lambda i: (i, 0, 0)),
            rows(160),
            rows(64),
        ],
        out_specs=(cols, rows(160), rows(64)),
        compiler_params=pltpu.CompilerParams(vmem_limit_bytes=56 * 2**20),
        name="apply_update",
    )(buf, ob, wide, ortho, q)


def whole_step(acts, out_grad, momentum, q_basis):
    any_space = pl.BlockSpec(memory_space=pl.ANY)
    in_hbm = pl.BlockSpec(memory_space=pltpu.HBM)
    in_vmem = pl.BlockSpec(memory_space=pltpu.VMEM)
    copies = 120
    vm = pltpu.VMEM
    scratch = [
        vm((1024, 640), BF16),
        vm((4, 640, 256), BF16),
        vm((640, 2048), F32),
        vm((8, 256, 256), F32),
        vm((2048, 256), BF16),
        vm((2048, 256), BF16),
        vm((4, 256, 256), F32),
        vm((4, 256, 256), BF16),
        vm((4, 256, 256), BF16),
        vm((4, 256, 2048), BF16),
        vm((128, 256), F32),
        vm((2, 640, 128), F32),
        vm((3, 2, 160, 128), F32),
        vm((2, 160, 128), F32),
        vm((2, 160, 128), F32),
        vm((7, 40, 128), F32),
        vm((40, 128), F32),
        vm((2, 640, 128), F32),
        vm((2048, 640), BF16),
        vm((2048, 640), BF16),
        vm((640, 256), BF16),
        vm((640, 256), BF16),
        vm((256, 256), F32),
        vm((8, 32, 256), F32),
        vm((32, 256), F32),
        vm((256, 256), F32),
        vm((256, 256), F32),
        vm((4, 2, 256, 256), F32),
        vm((4, 256, 256), F32),
        vm((4, 2, 128, 256), F32),
        vm((3, 128, 256), F32),
        vm((128, 256), F32),
        vm((128, 256), F32),
        vm((3, 4, 32, 256), F32),
        vm((4, 32, 256), F32),
        vm((4, 32, 256), F32),
        vm((3, 32, 256), F32),
        vm((3, 32, 256), F32),
        vm((64, 256), F32),
        vm((7, 8, 256), F32),
        vm((8, 256), F32),
        vm((64, 256), F32),
        vm((2, 128, 256), F32),
        vm((8, 256, 256), BF16),
        vm((8, 8, 256), F32),
        pltpu.SemaphoreType.DMA((copies,)),
        pltpu.SemaphoreType.DMA((copies,)),
        pltpu.SemaphoreType.DMA((12,)),
    ]
    outs = pl.pallas_call(
        step_kernel,
        out_shape=(
            jax.ShapeDtypeStruct((640, 2048), F32),
            jax.ShapeDtypeStruct((640, 256), BF16),
            jax.ShapeDtypeStruct((8, 256, 256), BF16),
            jax.ShapeDtypeStruct((640, 256), F32),
            jax.ShapeDtypeStruct((256, 256), F32),
        ),
        in_specs=[in_hbm] * 4,
        out_specs=(any_space, in_vmem, in_vmem, in_vmem, in_vmem),
        scratch_shapes=scratch,
        compiler_params=pltpu.CompilerParams(
            collective_id=0, has_side_effects=True, vmem_limit_bytes=60 * 2**20
        ),
        name="whole_step",
    )(acts, out_grad, momentum, q_basis)
    return apply_update(*outs)


def solution(mesh):
    split = Mesh(mesh.devices.reshape(4, 8, 4, 2), ("dp_0", "dp_1", "tensor_0", "tensor_1"))
    return jax.shard_map(
        whole_step,
        mesh=split,
        in_specs=(P(DP, TENSOR), P(DP_TENSOR, None), P(DP_TENSOR, None), P(TENSOR, None)),
        out_specs=(P(DP_TENSOR, None), P(TENSOR, None), P(TENSOR, None)),
        check_vma=False,
    )
```

```python
import jax
import jax.numpy as jnp
from jax import lax
from jax.experimental import pallas as pl
from jax.experimental.pallas import tpu as pltpu
from jax.sharding import Mesh
from jax.sharding import PartitionSpec as P

DP = ("dp_0", "dp_1")
TENSOR = ("tensor_0", "tensor_1")
DP_TENSOR = ("dp_0", "dp_1", "tensor_0", "tensor_1")
HIGH = lax.Precision.HIGHEST
F32, BF16 = jnp.float32, jnp.bfloat16
MESH = pl.DeviceIdType.MESH


def halves(value):
    high = value.astype(BF16)
    return high, (value - high.astype(F32)).astype(BF16)


def mxu(a, b):
    return lax.dot_general(a, b, (((1,), (0,)), ((), ())), preferred_element_type=F32)


class Place:
    def __init__(self):
        self.y, self.z = lax.axis_index("dp_0"), lax.axis_index("dp_1")
        self.x, self.c = lax.axis_index("tensor_0"), lax.axis_index("tensor_1")
        step = 1 - 2 * self.c
        self.sib = 1 - self.c
        self.xp, self.xm = lax.rem(self.x + step + 4, 4), lax.rem(self.x - step + 4, 4)
        self.yp, self.ym = lax.rem(self.y + step + 4, 4), lax.rem(self.y - step + 4, 4)
        self.xo, self.yo = lax.rem(self.x + 2, 4), lax.rem(self.y + 2, 4)

    def tensor_peers(self):
        peers = [({"tensor_1": self.sib}, 2 * self.x + self.sib)]
        for n in range(1, 4):
            there = lax.rem(self.x + n, 4)
            for core in (self.c, self.sib):
                peers.append(({"tensor_0": there, "tensor_1": core}, 2 * there + core))
        return peers

    def zk(self, k):
        return lax.rem(self.z + k, 8)


def greet(me):
    barrier = pltpu.get_barrier_semaphore()
    targets = [peer for peer, _ in me.tensor_peers()]
    targets += [{"dp_0": me.yp}, {"dp_0": me.ym}, {"dp_0": me.yo}]
    targets += [{"dp_1": me.zk(k)} for k in range(1, 8)]
    for target in targets:
        pl.semaphore_signal(barrier, inc=1, device_id=target, device_id_type=MESH)
    pl.semaphore_wait(barrier, len(targets))


class Links:
    def __init__(self, send, recv):
        self.send, self.recv, self.used, self.sent = send, recv, 0, []

    def to(self, src, dst, target):
        copy = pltpu.make_async_remote_copy(
            src_ref=src,
            dst_ref=dst,
            send_sem=self.send.at[self.used],
            recv_sem=self.recv.at[self.used],
            device_id=target,
            device_id_type=MESH,
        )
        self.used += 1
        copy.start()
        self.sent.append(copy)
        return copy

    def finish(self):
        for copy in self.sent:
            copy.wait_send()


class Gather:
    def __init__(self, me, links, own, slot):
        self.me, self.links, self.slot = me, links, slot
        here = slot(me.x, me.c)
        self.a = links.to(own, here, {"tensor_0": me.xp})
        self.b = links.to(own, here, {"tensor_0": me.xm})
        self.s0 = links.to(own, here, {"tensor_1": me.sib})

    def first(self):
        me = self.me
        self.a.wait_recv()
        block = self.slot(me.xm, me.c)
        self.f = self.links.to(block, block, {"tensor_0": me.xp})
        self.s1 = self.links.to(block, block, {"tensor_1": me.sib})

    def second(self):
        me = self.me
        self.b.wait_recv()
        block = self.slot(me.xp, me.c)
        self.s2 = self.links.to(block, block, {"tensor_1": me.sib})

    def third(self):
        me = self.me
        self.f.wait_recv()
        block = self.slot(me.xo, me.c)
        self.s3 = self.links.to(block, block, {"tensor_1": me.sib})

    def rest(self):
        for copy in (self.s0, self.s1, self.s2, self.s3):
            copy.wait_recv()


class RingSum:
    def __init__(self, links, axis, places, src, came, stage):
        own, plus, minus, far = places
        self.links, self.axis, self.src = links, axis, src
        self.own, self.plus, self.came, self.stage = own, plus, came, stage
        self.far = links.to(src(far), came.at[0], {axis: plus})
        self.near = links.to(src(minus), came.at[1], {axis: minus})

    def middle(self):
        self.far.wait_recv()
        self.stage[...] = self.came[0] + self.src(self.plus)[...]
        self.last = self.links.to(self.stage, self.came.at[2], {self.axis: self.plus})

    def total(self):
        self.near.wait_recv()
        self.last.wait_recv()
        return self.src(self.own)[...] + self.came[1] + self.came[2]


class RingSpread:
    def __init__(self, links, axis, places, slot):
        own, plus, minus, _ = places
        self.links, self.axis, self.plus = links, axis, plus
        self.from_minus = slot(minus)
        self.up = links.to(slot(own), slot(own), {axis: plus})
        self.down = links.to(slot(own), slot(own), {axis: minus})

    def middle(self):
        self.up.wait_recv()
        self.far = self.links.to(self.from_minus, self.from_minus, {self.axis: self.plus})

    def finish(self):
        self.down.wait_recv()
        self.far.wait_recv()


class DirectSum:
    def __init__(self, links, axis, places, src, came):
        own, *others = places
        self.mine, self.came = src(own), came
        self.copies = [
            links.to(src(there), came.at[n], {axis: there}) for n, there in enumerate(others)
        ]

    def total(self):
        for copy in self.copies:
            copy.wait_recv()
        return self.mine[...] + self.came[0] + self.came[1] + self.came[2]


class HalfGathers:
    def __init__(self, me, links, own, slot):
        self.parts = [
            Gather(me, links, own(p), lambda x, c, p=p: slot(x, c, p)) for p in range(2)
        ]

    def first(self):
        for part in self.parts:
            part.first()

    def second(self):
        for part in self.parts:
            part.second()

    def third(self):
        for part in self.parts:
            part.third()

    def sibling(self, n):
        for part in self.parts:
            getattr(part, "s%d" % n).wait_recv()

    def rest(self):
        for n in range(4):
            self.sibling(n)


def three(a, b, dims=((1,), (0,))):
    dot = lambda p, q: lax.dot_general(p, q, (dims, ((), ())), preferred_element_type=F32)
    return dot(a[0], b[0]) + dot(a[0], b[1]) + dot(a[1], b[0])


def rows_at(start, size, unit=8):
    return pl.ds(pl.multiple_of(start, unit), size)


def eliminate(d):
    lane = lax.broadcasted_iota(jnp.int32, (64, 128), 1)
    row = lax.broadcasted_iota(jnp.int32, (64, 128), 0)
    e = jnp.where(lane < 64, d, jnp.where(lane - 64 == row, 1.0, 0.0).astype(F32))

    def panel(p, e):
        live = 64 - 8 * p
        for first in range(0, 8, 8):
            cols = [jnp.broadcast_to(e[:, j : j + 1], (64, 128)) for j in range(first, first + 8)]
            for n, col in enumerate(cols):
                j = first + n
                weight = pltpu.reciprocal(col[j : j + 1])
                factor = jnp.where((row > j) & (row < live), col, 0.0) * weight
                e = e - factor * e[j : j + 1]
                for m in range(n + 1, 8):
                    cols[m] = cols[m] - factor * col[first + m : first + m + 1]
        e = pltpu.roll(e, 120, 1)
        return jnp.concatenate([e[8:], e[:8]], axis=0)

    e = lax.fori_loop(0, 8, panel, e)
    v = e[:, :64]
    diag = jnp.sum(jnp.where(lane - 64 == row, e, 0.0), axis=1, keepdims=True)
    return v * lax.rsqrt(diag)


def exact(a, b, dims=((1,), (0,))):
    return lax.dot_general(a, b, (dims, ((), ())), precision=HIGH, preferred_element_type=F32)


def factor_block(k, a, inv):
    rows = slice(64 * k, 64 * k + 64)
    block = a[rows, 128 * (k // 2) : 128 * (k // 2) + 128]
    if k % 2:
        block = pltpu.roll(block, 64, 1)
    v = eliminate(block)
    inv_row = exact(v, inv[rows, :])
    inv[rows, :] = inv_row
    if k < 3:
        u = exact(v, a[rows, :])
        below = u.T[64 * (k + 1) :, :]
        rest = slice(64 * (k + 1), 256)
        a[rest, :] = a[rest, :] - exact(below, u)
        inv[rest, :] = inv[rest, :] - exact(below, inv_row)


def step_kernel(
    acts, og, mom, q, buf_out, ob, wide_out, ortho_out, q_out,
    actsv, acts_t, buf, qg, qh, ql, yg, yh, yl, ogg, y_own,
    part, r_left, s1, chunk, zr, zs, full,
    bth, btl, lh, ll, gram, gram_r, gram_s, a, inv,
    cc, c_sib, c_sum, rx, sx, tx, ry, sy, ty, rxy, ryx,
    rest, zr2, zs2, all_z, own_right, wide, sq,
    send, recv, local,
):
    me = Place()
    links = Links(send, recv)
    own_q = qg.at[me.x * 2 + me.c]
    own_rows = pl.ds(pl.multiple_of(me.c * 128, 128), 128)
    own_og = ogg.at[me.x, own_rows]
    loads = [
        pltpu.make_async_copy(q, own_q, local.at[0]),
        pltpu.make_async_copy(og, own_og, local.at[1]),
        pltpu.make_async_copy(acts, actsv, local.at[2]),
        pltpu.make_async_copy(mom, buf, local.at[3]),
    ]
    for load in loads:
        load.start()
    greet(me)
    gq = HalfGathers(
        me,
        links,
        lambda p: q.at[pl.ds(128 * p, 128)],
        lambda x, c, p: qg.at[x * 2 + c, pl.ds(128 * p, 128)],
    )
    gq.first()
    gq.second()
    loads[2].wait()
    for j in range(4):
        acts_t[j] = actsv[256 * j : 256 * (j + 1), :].T
    loads[0].wait()
    loads[1].wait()
    loads[3].wait()
    own = ogg.at[me.x, own_rows]

    def take(x, c, first=False):
        b = 2 * x + c
        rows = rows_at(b * 256, 256, 256)
        high, low = halves(qg[b])
        qh[rows, :], ql[rows, :] = high, low
        lhs = own[:, rows]
        share = mxu(lhs, high) + mxu(lhs, low)
        y_own[...] = share if first else y_own[...] + share

    take(me.x, me.c, True)
    take(me.xm, me.c)
    take(me.xp, me.c)
    gq.sibling(0)
    take(me.x, me.sib)
    gq.third()
    take(me.xo, me.c)
    gq.sibling(1)
    take(me.xp, me.sib)
    gq.sibling(2)
    take(me.xm, me.sib)
    gq.sibling(3)
    take(me.xo, me.sib)
    yg[me.x, own_rows, :] = y_own[...]
    own_y = yg.at[me.x, own_rows]
    gy = Gather(me, links, own_y, lambda x, c: yg.at[x, pl.ds(pl.multiple_of(c * 128, 128), 128)])

    def momentum_part(t):
        rows = rows_at(t * 128, 128)
        share = three(halves(buf[rows, :]), (qh[...], ql[...]))
        for half in range(2):
            part[half, rows, :] = share[:, 128 * half : 128 * half + 128]

    pl.loop(0, 3)(momentum_part)
    gy.first()
    gy.second()
    pl.loop(3, 5)(momentum_part)
    gy.third()
    gy.rest()
    go = Gather(
        me, links, og, lambda x, c: ogg.at[x, pl.ds(pl.multiple_of(c * 128, 128), 128)]
    )
    for j in range(4):
        high, low = halves(yg[j])
        yh[j], yl[j] = high, low

    @pl.loop(0, 5)
    def _(t):
        rows = pl.ds(pl.multiple_of(t * 128, 128), 128)
        acc = jnp.zeros((128, 256), F32)
        for j in range(4):
            lhs = acts_t[j, rows, :]
            acc += mxu(lhs, yh[j]) + mxu(lhs, yl[j])
        for half in range(2):
            piece = acc[:, 128 * half : 128 * half + 128]
            part[half, rows, :] = (0.95 * part[half, rows, :] + piece) * (1 / 32)

    def of_y(ref, y):
        return ref.at[:, pl.ds(pl.multiple_of(y * 160, 32), 160)]

    ys, xs = (me.y, me.yp, me.ym, me.yo), (me.x, me.xp, me.xm, me.xo)
    ring = RingSum(links, "dp_0", ys, lambda y: of_y(part, y), r_left, s1)
    ring.middle()
    chunk[...] = ring.total()

    def z_rows(z):
        return z // 4, pl.multiple_of(lax.rem(z, 4) * 40, 8)

    came = []
    for k in range(1, 8):
        half, row = z_rows(me.zk(k))
        came.append(
            links.to(chunk.at[half, pl.ds(row, 40)], zr.at[k - 1], {"dp_1": me.zk(k)})
        )
    go.first()
    go.second()
    half, row = z_rows(me.z)
    for copy in came:
        copy.wait_recv()
    total = chunk[half, pl.ds(row, 40), :]
    for k in range(7):
        total += zr[k]
    zs[...] = total
    spot = full.at[half, pl.ds(pl.multiple_of(me.y * 160 + row, 8), 40)]
    came = [links.to(zs, spot, {"dp_1": me.zk(k)}) for k in range(1, 8)]
    spot[...] = total
    go.third()
    for copy in came:
        copy.wait_recv()
    spread = RingSpread(links, "dp_0", ys, lambda y: of_y(full, y))

    def buffer_part(n):
        cols = rows_at(n * 256, 256, 256)
        acc = 0.95 * buf[:, cols]
        for j in range(4):
            acc += mxu(acts_t[j], ogg[j, :, cols])
        buf[:, cols] = acc
        bth[cols, :], btl[cols, :] = halves(acc.T)

    go.rest()
    pl.loop(0, 4)(buffer_part)
    spread.middle()
    pl.loop(4, 8)(buffer_part)
    store = pltpu.make_async_copy(buf, buf_out, local.at[4])
    store.start()
    spread.finish()
    lt = []
    for half in range(2):
        cols = slice(128 * half, 128 * half + 128)
        lh[:, cols], ll[:, cols] = halves(full[half])
        lt.append(full[half].T)
    left = lh[...], ll[...]
    gram[...] = three(halves(jnp.concatenate(lt, axis=0)), left)

    def product_with(core):
        @pl.loop(0, 4)
        def _(n):
            rows = rows_at((2 * n + core) * 256, 256, 256)
            cc[n, core] = three((bth[rows, :], btl[rows, :]), (lh[...], ll[...]))

    index = 2 * me.x + me.c
    gram_in = []
    for peer, there in me.tensor_peers():
        gram_in.append(links.to(gram.at[rows_at(there * 32, 32)], gram_r.at[index], peer))
    gram_r[index] = gram[rows_at(index * 32, 32), :]
    product_with(me.sib)
    swap = links.to(cc.at[:, me.sib], c_sib, {"tensor_1": me.sib})
    for copy in gram_in:
        copy.wait_recv()
    total = gram_r[0]
    for b in range(1, 8):
        total += gram_r[b]
    gram_s[...] = total
    gram_rows = a.at[rows_at(index * 32, 32)]
    gram_in = [links.to(gram_s, gram_rows, peer) for peer, _ in me.tensor_peers()]
    gram_rows[...] = total
    product_with(me.c)
    swap.wait_recv()
    c_sum[...] = cc[:, me.c].reshape(4, 2, 128, 256) + c_sib[...].reshape(4, 2, 128, 256)
    x_first = RingSum(links, "tensor_0", xs, lambda x: c_sum.at[x, 0], rx, sx)
    y_first = RingSum(
        links, "dp_0", ys, lambda y: c_sum.at[:, 1, rows_at(y * 32, 32)], ry, sy
    )
    same = lax.broadcasted_iota(jnp.int32, (256, 256), 0) == lax.broadcasted_iota(
        jnp.int32, (256, 256), 1
    )
    inv[...] = jnp.where(same, 1.0, 0.0).astype(F32)
    for copy in gram_in:
        copy.wait_recv()
    factor_block(0, a, inv)
    y_first.middle()
    x_first.middle()
    factor_block(1, a, inv)
    tx[...] = x_first.total()
    then_y = DirectSum(links, "dp_0", ys, lambda y: tx.at[rows_at(y * 32, 32)], ryx)
    ty[...] = y_first.total()
    then_x = DirectSum(links, "tensor_0", xs, lambda x: ty.at[x], rxy)
    factor_block(2, a, inv)
    rest[:32, :] = then_y.total()
    rest[32:, :] = then_x.total()
    came = [
        links.to(rest.at[rows_at(me.zk(k) * 8, 8)], zr2.at[k - 1], {"dp_1": me.zk(k)})
        for k in range(1, 8)
    ]
    factor_block(3, a, inv)
    for copy in came:
        copy.wait_recv()
    total = rest[rows_at(me.z * 8, 8), :]
    for k in range(7):
        total += zr2[k]
    total = total * (1 / 32)
    zs2[...] = total
    spot = all_z.at[rows_at(me.z * 8, 8)]
    came = [links.to(zs2, spot, {"dp_1": me.zk(k)}) for k in range(1, 8)]
    spot[...] = total
    inverse = halves(inv[...])
    across = ((1,), (1,))
    for copy in came:
        copy.wait_recv()
    mine = three(halves(all_z[...]), inverse, across)
    own_right[0, rows_at(me.y * 32, 32), :] = mine[:32]
    own_right[1, rows_at(me.y * 32, 32), :] = mine[32:]
    own_part = own_right.at[:, rows_at(me.y * 32, 32)]
    came = [links.to(own_part, own_part, {"dp_0": there}) for there in ys[1:]]
    ortho = three((lh[...], ll[...]), inverse, across)
    ortho_out[...] = ortho
    ob[...] = (ortho * 0.05).astype(BF16)
    for copy in came:
        copy.wait_recv()
    wide[index, :128, :] = own_right[0].astype(BF16)
    wide[index, 128:, :] = own_right[1].astype(BF16)
    gw = HalfGathers(
        me,
        links,
        lambda p: wide.at[index, pl.ds(128 * p, 128)],
        lambda x, c, p: wide.at[2 * x + c, pl.ds(128 * p, 128)],
    )
    values = own_right[...].reshape(256, 256)
    sq[index] = jnp.broadcast_to(jnp.sum(values * values, axis=0, keepdims=True), (8, 256))
    mark = sq.at[index]
    came = [links.to(mark, mark, peer) for peer, _ in me.tensor_peers()]
    gw.first()
    gw.second()
    for copy in came:
        copy.wait_recv()
    squares = sq[0]
    for b in range(1, 8):
        squares += sq[b]
    q_out[...] = values * lax.rsqrt(squares[:1] + 1e-06)
    gw.third()
    gw.rest()
    wide_out[...] = wide[...]
    store.wait()
    links.finish()


def apply_kernel(buf, ob, wide, ortho, q, new_out, ortho_out, q_out):
    for b in range(2):
        cols = slice(256 * b, 256 * b + 256)
        update = lax.dot_general(
            ob[...], wide[b], (((1,), (1,)), ((), ())), preferred_element_type=F32
        )
        new_out[:, cols] = buf[:, cols] - update
    ortho_out[...] = ortho[...]
    q_out[...] = q[...]


def apply_update(buf, ob, wide, ortho, q):
    def rows(height):
        return pl.BlockSpec((height, 256), lambda i: (i, 0))

    cols = pl.BlockSpec((640, 512), lambda i: (0, i))
    return pl.pallas_call(
        apply_kernel,
        grid=(4,),
        out_shape=(
            jax.ShapeDtypeStruct((640, 2048), F32),
            jax.ShapeDtypeStruct((640, 256), F32),
            jax.ShapeDtypeStruct((256, 256), F32),
        ),
        in_specs=[
            cols,
            pl.BlockSpec((640, 256), lambda i: (0, 0)),
            pl.BlockSpec((2, 256, 256), lambda i: (i, 0, 0)),
            rows(160),
            rows(64),
        ],
        out_specs=(cols, rows(160), rows(64)),
        compiler_params=pltpu.CompilerParams(vmem_limit_bytes=24 * 2**20),
        name="apply_update",
    )(buf, ob, wide, ortho, q)


def whole_step(acts, out_grad, momentum, q_basis):
    any_space = pl.BlockSpec(memory_space=pl.ANY)
    in_hbm = pl.BlockSpec(memory_space=pltpu.HBM)
    in_vmem = pl.BlockSpec(memory_space=pltpu.VMEM)
    copies = 120
    vm = pltpu.VMEM
    scratch = [
        vm((1024, 640), BF16),
        vm((4, 640, 256), BF16),
        vm((640, 2048), F32),
        vm((8, 256, 256), F32),
        vm((2048, 256), BF16),
        vm((2048, 256), BF16),
        vm((4, 256, 256), F32),
        vm((4, 256, 256), BF16),
        vm((4, 256, 256), BF16),
        vm((4, 256, 2048), BF16),
        vm((128, 256), F32),
        vm((2, 640, 128), F32),
        vm((3, 2, 160, 128), F32),
        vm((2, 160, 128), F32),
        vm((2, 160, 128), F32),
        vm((7, 40, 128), F32),
        vm((40, 128), F32),
        vm((2, 640, 128), F32),
        vm((2048, 640), BF16),
        vm((2048, 640), BF16),
        vm((640, 256), BF16),
        vm((640, 256), BF16),
        vm((256, 256), F32),
        vm((8, 32, 256), F32),
        vm((32, 256), F32),
        vm((256, 256), F32),
        vm((256, 256), F32),
        vm((4, 2, 256, 256), F32),
        vm((4, 256, 256), F32),
        vm((4, 2, 128, 256), F32),
        vm((3, 128, 256), F32),
        vm((128, 256), F32),
        vm((128, 256), F32),
        vm((3, 4, 32, 256), F32),
        vm((4, 32, 256), F32),
        vm((4, 32, 256), F32),
        vm((3, 32, 256), F32),
        vm((3, 32, 256), F32),
        vm((64, 256), F32),
        vm((7, 8, 256), F32),
        vm((8, 256), F32),
        vm((64, 256), F32),
        vm((2, 128, 256), F32),
        vm((8, 256, 256), BF16),
        vm((8, 8, 256), F32),
        pltpu.SemaphoreType.DMA((copies,)),
        pltpu.SemaphoreType.DMA((copies,)),
        pltpu.SemaphoreType.DMA((12,)),
    ]
    outs = pl.pallas_call(
        step_kernel,
        out_shape=(
            pltpu.VMEM((640, 2048), F32),
            pltpu.VMEM((640, 256), BF16),
            pltpu.VMEM((8, 256, 256), BF16),
            pltpu.VMEM((640, 256), F32),
            pltpu.VMEM((256, 256), F32),
        ),
        in_specs=[in_hbm] * 4,
        out_specs=(in_vmem, in_vmem, in_vmem, in_vmem, in_vmem),
        scratch_shapes=scratch,
        compiler_params=pltpu.CompilerParams(
            collective_id=0, has_side_effects=True, vmem_limit_bytes=56 * 2**20
        ),
        name="whole_step",
    )(acts, out_grad, momentum, q_basis)
    return apply_update(*outs)


def solution(mesh):
    split = Mesh(mesh.devices.reshape(4, 8, 4, 2), ("dp_0", "dp_1", "tensor_0", "tensor_1"))
    return jax.shard_map(
        whole_step,
        mesh=split,
        in_specs=(P(DP, TENSOR), P(DP_TENSOR, None), P(DP_TENSOR, None), P(TENSOR, None)),
        out_specs=(P(DP_TENSOR, None), P(TENSOR, None), P(TENSOR, None)),
        check_vma=False,
    )
```

```python
import jax
import jax.numpy as jnp
from jax import lax
from jax.experimental import pallas as pl
from jax.experimental.pallas import tpu as pltpu
from jax.sharding import Mesh
from jax.sharding import PartitionSpec as P

DP = ("dp_0", "dp_1")
TENSOR = ("tensor_0", "tensor_1")
DP_TENSOR = ("dp_0", "dp_1", "tensor_0", "tensor_1")
HIGH = lax.Precision.HIGHEST
F32, BF16 = jnp.float32, jnp.bfloat16
MESH = pl.DeviceIdType.MESH


def halves(value):
    high = value.astype(BF16)
    return high, (value - high.astype(F32)).astype(BF16)


def mxu(a, b):
    return lax.dot_general(a, b, (((1,), (0,)), ((), ())), preferred_element_type=F32)


class Place:
    def __init__(self):
        self.y, self.z = lax.axis_index("dp_0"), lax.axis_index("dp_1")
        self.x, self.c = lax.axis_index("tensor_0"), lax.axis_index("tensor_1")
        step = 1 - 2 * self.c
        self.sib = 1 - self.c
        self.xp, self.xm = lax.rem(self.x + step + 4, 4), lax.rem(self.x - step + 4, 4)
        self.yp, self.ym = lax.rem(self.y + step + 4, 4), lax.rem(self.y - step + 4, 4)
        self.xo, self.yo = lax.rem(self.x + 2, 4), lax.rem(self.y + 2, 4)

    def tensor_peers(self):
        peers = [({"tensor_1": self.sib}, 2 * self.x + self.sib)]
        for n in range(1, 4):
            there = lax.rem(self.x + n, 4)
            for core in (self.c, self.sib):
                peers.append(({"tensor_0": there, "tensor_1": core}, 2 * there + core))
        return peers

    def zk(self, k):
        return lax.rem(self.z + k, 8)


def greet(me):
    barrier = pltpu.get_barrier_semaphore()
    targets = [peer for peer, _ in me.tensor_peers()]
    targets += [{"dp_0": me.yp}, {"dp_0": me.ym}, {"dp_0": me.yo}]
    targets += [{"dp_1": me.zk(k)} for k in range(1, 8)]
    for target in targets:
        pl.semaphore_signal(barrier, inc=1, device_id=target, device_id_type=MESH)
    pl.semaphore_wait(barrier, len(targets))


class Links:
    def __init__(self, send, recv):
        self.send, self.recv, self.used, self.sent = send, recv, 0, []

    def to(self, src, dst, target):
        copy = pltpu.make_async_remote_copy(
            src_ref=src,
            dst_ref=dst,
            send_sem=self.send.at[self.used],
            recv_sem=self.recv.at[self.used],
            device_id=target,
            device_id_type=MESH,
        )
        self.used += 1
        copy.start()
        self.sent.append(copy)
        return copy

    def finish(self):
        for copy in self.sent:
            copy.wait_send()


class Gather:
    def __init__(self, me, links, own, slot):
        self.me, self.links, self.slot = me, links, slot
        here = slot(me.x, me.c)
        self.a = links.to(own, here, {"tensor_0": me.xp})
        self.b = links.to(own, here, {"tensor_0": me.xm})
        self.s0 = links.to(own, here, {"tensor_1": me.sib})

    def first(self):
        me = self.me
        self.a.wait_recv()
        block = self.slot(me.xm, me.c)
        self.f = self.links.to(block, block, {"tensor_0": me.xp})
        self.s1 = self.links.to(block, block, {"tensor_1": me.sib})

    def second(self):
        me = self.me
        self.b.wait_recv()
        block = self.slot(me.xp, me.c)
        self.s2 = self.links.to(block, block, {"tensor_1": me.sib})

    def third(self):
        me = self.me
        self.f.wait_recv()
        block = self.slot(me.xo, me.c)
        self.s3 = self.links.to(block, block, {"tensor_1": me.sib})

    def rest(self):
        for copy in (self.s0, self.s1, self.s2, self.s3):
            copy.wait_recv()


class RingSum:
    def __init__(self, links, axis, places, src, came, stage):
        own, plus, minus, far = places
        self.links, self.axis, self.src = links, axis, src
        self.own, self.plus, self.came, self.stage = own, plus, came, stage
        self.far = links.to(src(far), came.at[0], {axis: plus})
        self.near = links.to(src(minus), came.at[1], {axis: minus})

    def middle(self):
        self.far.wait_recv()
        self.stage[...] = self.came[0] + self.src(self.plus)[...]
        self.last = self.links.to(self.stage, self.came.at[2], {self.axis: self.plus})

    def total(self):
        self.near.wait_recv()
        self.last.wait_recv()
        return self.src(self.own)[...] + self.came[1] + self.came[2]


class RingSpread:
    def __init__(self, links, axis, places, slot):
        own, plus, minus, _ = places
        self.links, self.axis, self.plus = links, axis, plus
        self.from_minus = slot(minus)
        self.up = links.to(slot(own), slot(own), {axis: plus})
        self.down = links.to(slot(own), slot(own), {axis: minus})

    def middle(self):
        self.up.wait_recv()
        self.far = self.links.to(self.from_minus, self.from_minus, {self.axis: self.plus})

    def finish(self):
        self.down.wait_recv()
        self.far.wait_recv()


class DirectSum:
    def __init__(self, links, axis, places, src, came):
        own, *others = places
        self.mine, self.came = src(own), came
        self.copies = [
            links.to(src(there), came.at[n], {axis: there}) for n, there in enumerate(others)
        ]

    def total(self):
        for copy in self.copies:
            copy.wait_recv()
        return self.mine[...] + self.came[0] + self.came[1] + self.came[2]


class HalfGathers:
    def __init__(self, me, links, own, slot):
        self.parts = [
            Gather(me, links, own(p), lambda x, c, p=p: slot(x, c, p)) for p in range(2)
        ]

    def first(self):
        for part in self.parts:
            part.first()

    def second(self):
        for part in self.parts:
            part.second()

    def third(self):
        for part in self.parts:
            part.third()

    def sibling(self, n):
        for part in self.parts:
            getattr(part, "s%d" % n).wait_recv()

    def rest(self):
        for n in range(4):
            self.sibling(n)


def three(a, b, dims=((1,), (0,))):
    dot = lambda p, q: lax.dot_general(p, q, (dims, ((), ())), preferred_element_type=F32)
    return dot(a[0], b[0]) + dot(a[0], b[1]) + dot(a[1], b[0])


def rows_at(start, size, unit=8):
    return pl.ds(pl.multiple_of(start, unit), size)


def eliminate(d):
    lane = lax.broadcasted_iota(jnp.int32, (64, 128), 1)
    row = lax.broadcasted_iota(jnp.int32, (64, 128), 0)
    e = jnp.where(lane < 64, d, jnp.where(lane - 64 == row, 1.0, 0.0).astype(F32))

    def panel(p, e):
        live = 64 - 8 * p
        for first in range(0, 8, 8):
            cols = [jnp.broadcast_to(e[:, j : j + 1], (64, 128)) for j in range(first, first + 8)]
            for n, col in enumerate(cols):
                j = first + n
                weight = pltpu.reciprocal(col[j : j + 1])
                factor = jnp.where((row > j) & (row < live), col, 0.0) * weight
                e = e - factor * e[j : j + 1]
                for m in range(n + 1, 8):
                    cols[m] = cols[m] - factor * col[first + m : first + m + 1]
        e = pltpu.roll(e, 120, 1)
        return jnp.concatenate([e[8:], e[:8]], axis=0)

    e = lax.fori_loop(0, 8, panel, e)
    v = e[:, :64]
    diag = jnp.sum(jnp.where(lane - 64 == row, e, 0.0), axis=1, keepdims=True)
    return v * lax.rsqrt(diag)


def exact(a, b, dims=((1,), (0,))):
    return lax.dot_general(a, b, (dims, ((), ())), precision=HIGH, preferred_element_type=F32)


def factor_block(k, a, inv):
    rows = slice(64 * k, 64 * k + 64)
    block = a[rows, 128 * (k // 2) : 128 * (k // 2) + 128]
    if k % 2:
        block = pltpu.roll(block, 64, 1)
    v = eliminate(block)
    inv_row = exact(v, inv[rows, :])
    inv[rows, :] = inv_row
    if k < 3:
        u = exact(v, a[rows, :])
        below = u.T[64 * (k + 1) :, :]
        rest = slice(64 * (k + 1), 256)
        a[rest, :] = a[rest, :] - exact(below, u)
        inv[rest, :] = inv[rest, :] - exact(below, inv_row)


def step_kernel(
    acts, og, mom, q, buf_out, ob, wide_out, ortho_out, q_out,
    actsv, acts_t, buf, qg, qh, ql, yg, yh, yl, ogg, y_own,
    part, r_left, s1, chunk, zr, zs, full,
    bth, btl, lh, ll, gram, gram_r, gram_s, a, inv,
    cc, c_sib, c_sum, rx, sx, tx, ry, sy, ty, rxy, ryx,
    rest, zr2, zs2, all_z, own_right, wide, sq,
    send, recv, local,
):
    me = Place()
    links = Links(send, recv)
    own_q = qg.at[me.x * 2 + me.c]
    own_rows = pl.ds(pl.multiple_of(me.c * 128, 128), 128)
    own_og = ogg.at[me.x, own_rows]
    loads = [
        pltpu.make_async_copy(q, own_q, local.at[0]),
        pltpu.make_async_copy(og, own_og, local.at[1]),
        pltpu.make_async_copy(acts, actsv, local.at[2]),
        pltpu.make_async_copy(mom, buf, local.at[3]),
    ]
    for load in loads:
        load.start()
    greet(me)
    gq = HalfGathers(
        me,
        links,
        lambda p: q.at[pl.ds(128 * p, 128)],
        lambda x, c, p: qg.at[x * 2 + c, pl.ds(128 * p, 128)],
    )
    gq.first()
    gq.second()
    loads[2].wait()
    for j in range(4):
        acts_t[j] = actsv[256 * j : 256 * (j + 1), :].T
    loads[0].wait()
    loads[1].wait()
    loads[3].wait()
    own = ogg.at[me.x, own_rows]

    def take(x, c, first=False):
        b = 2 * x + c
        rows = rows_at(b * 256, 256, 256)
        high, low = halves(qg[b])
        qh[rows, :], ql[rows, :] = high, low
        lhs = own[:, rows]
        share = mxu(lhs, high) + mxu(lhs, low)
        y_own[...] = share if first else y_own[...] + share

    take(me.x, me.c, True)
    take(me.xm, me.c)
    take(me.xp, me.c)
    gq.sibling(0)
    take(me.x, me.sib)
    gq.third()
    take(me.xo, me.c)
    gq.sibling(1)
    take(me.xp, me.sib)
    gq.sibling(2)
    take(me.xm, me.sib)
    gq.sibling(3)
    take(me.xo, me.sib)
    yg[me.x, own_rows, :] = y_own[...]
    def y_piece(x, c, p):
        return yg.at[x, rows_at(c * 128 + 64 * p, 64, 64)]

    gy = HalfGathers(me, links, lambda p: y_piece(me.x, me.c, p), y_piece)

    def momentum_part(t):
        rows = rows_at(t * 128, 128)
        share = three(halves(buf[rows, :]), (qh[...], ql[...]))
        for half in range(2):
            part[half, rows, :] = share[:, 128 * half : 128 * half + 128]

    pl.loop(0, 3)(momentum_part)
    gy.first()
    gy.second()
    pl.loop(3, 5)(momentum_part)
    gy.third()
    gy.rest()
    go = Gather(
        me, links, og, lambda x, c: ogg.at[x, pl.ds(pl.multiple_of(c * 128, 128), 128)]
    )
    for j in range(4):
        high, low = halves(yg[j])
        yh[j], yl[j] = high, low

    @pl.loop(0, 5)
    def _(t):
        rows = pl.ds(pl.multiple_of(t * 128, 128), 128)
        acc = jnp.zeros((128, 256), F32)
        for j in range(4):
            lhs = acts_t[j, rows, :]
            acc += mxu(lhs, yh[j]) + mxu(lhs, yl[j])
        for half in range(2):
            piece = acc[:, 128 * half : 128 * half + 128]
            part[half, rows, :] = (0.95 * part[half, rows, :] + piece) * (1 / 32)

    ys, xs = (me.y, me.yp, me.ym, me.yo), (me.x, me.xp, me.xm, me.xo)
    rings = [
        RingSum(
            links,
            "dp_0",
            ys,
            lambda y, h=h: part.at[h, rows_at(y * 160, 160, 32)],
            r_left.at[h],
            s1.at[h],
        )
        for h in range(2)
    ]
    for ring in rings:
        ring.middle()
    for h in range(2):
        chunk[h] = rings[h].total()

    def z_rows(z):
        return z // 4, pl.multiple_of(lax.rem(z, 4) * 40, 8)

    came = []
    for k in range(1, 8):
        half, row = z_rows(me.zk(k))
        came.append(
            links.to(chunk.at[half, pl.ds(row, 40)], zr.at[k - 1], {"dp_1": me.zk(k)})
        )
    go.first()
    go.second()
    half, row = z_rows(me.z)
    for copy in came:
        copy.wait_recv()
    total = chunk[half, pl.ds(row, 40), :]
    for k in range(7):
        total += zr[k]
    zs[...] = total
    spot = full.at[half, pl.ds(pl.multiple_of(me.y * 160 + row, 8), 40)]
    came = [links.to(zs, spot, {"dp_1": me.zk(k)}) for k in range(1, 8)]
    spot[...] = total
    go.third()
    for copy in came:
        copy.wait_recv()
    spreads = [
        RingSpread(links, "dp_0", ys, lambda y, h=h: full.at[h, rows_at(y * 160, 160, 32)])
        for h in range(2)
    ]

    def buffer_part(n):
        cols = rows_at(n * 256, 256, 256)
        acc = 0.95 * buf[:, cols]
        for j in range(4):
            acc += mxu(acts_t[j], ogg[j, :, cols])
        buf[:, cols] = acc
        bth[cols, :], btl[cols, :] = halves(acc.T)

    go.rest()
    pl.loop(0, 4)(buffer_part)
    for spread in spreads:
        spread.middle()
    pl.loop(4, 8)(buffer_part)
    store = pltpu.make_async_copy(buf, buf_out, local.at[4])
    store.start()
    for spread in spreads:
        spread.finish()
    lt = []
    for half in range(2):
        cols = slice(128 * half, 128 * half + 128)
        lh[:, cols], ll[:, cols] = halves(full[half])
        lt.append(full[half].T)
    left = lh[...], ll[...]
    gram[...] = three(halves(jnp.concatenate(lt, axis=0)), left)

    def product_with(core):
        @pl.loop(0, 4)
        def _(n):
            rows = rows_at((2 * n + core) * 256, 256, 256)
            cc[n, core] = three((bth[rows, :], btl[rows, :]), (lh[...], ll[...]))

    index = 2 * me.x + me.c
    gram_in = []
    for peer, there in me.tensor_peers():
        gram_in.append(links.to(gram.at[rows_at(there * 32, 32)], gram_r.at[index], peer))
    gram_r[index] = gram[rows_at(index * 32, 32), :]
    product_with(me.sib)
    swap = links.to(cc.at[:, me.sib], c_sib, {"tensor_1": me.sib})
    for copy in gram_in:
        copy.wait_recv()
    total = gram_r[0]
    for b in range(1, 8):
        total += gram_r[b]
    gram_s[...] = total
    gram_rows = a.at[rows_at(index * 32, 32)]
    gram_in = [links.to(gram_s, gram_rows, peer) for peer, _ in me.tensor_peers()]
    gram_rows[...] = total
    product_with(me.c)
    swap.wait_recv()
    c_sum[...] = cc[:, me.c].reshape(4, 2, 128, 256) + c_sib[...].reshape(4, 2, 128, 256)
    x_first = RingSum(links, "tensor_0", xs, lambda x: c_sum.at[x, 0], rx, sx)
    y_first = RingSum(
        links, "dp_0", ys, lambda y: c_sum.at[:, 1, rows_at(y * 32, 32)], ry, sy
    )
    same = lax.broadcasted_iota(jnp.int32, (256, 256), 0) == lax.broadcasted_iota(
        jnp.int32, (256, 256), 1
    )
    inv[...] = jnp.where(same, 1.0, 0.0).astype(F32)
    for copy in gram_in:
        copy.wait_recv()
    factor_block(0, a, inv)
    y_first.middle()
    x_first.middle()
    factor_block(1, a, inv)
    tx[...] = x_first.total()
    then_y = DirectSum(links, "dp_0", ys, lambda y: tx.at[rows_at(y * 32, 32)], ryx)
    ty[...] = y_first.total()
    then_x = DirectSum(links, "tensor_0", xs, lambda x: ty.at[x], rxy)
    factor_block(2, a, inv)
    rest[:32, :] = then_y.total()
    rest[32:, :] = then_x.total()
    came = [
        links.to(rest.at[rows_at(me.zk(k) * 8, 8)], zr2.at[k - 1], {"dp_1": me.zk(k)})
        for k in range(1, 8)
    ]
    factor_block(3, a, inv)
    for copy in came:
        copy.wait_recv()
    total = rest[rows_at(me.z * 8, 8), :]
    for k in range(7):
        total += zr2[k]
    total = total * (1 / 32)
    zs2[...] = total
    spot = all_z.at[rows_at(me.z * 8, 8)]
    came = [links.to(zs2, spot, {"dp_1": me.zk(k)}) for k in range(1, 8)]
    spot[...] = total
    inverse = halves(inv[...])
    across = ((1,), (1,))
    for copy in came:
        copy.wait_recv()
    mine = three(halves(all_z[...]), inverse, across)
    own_right[0, rows_at(me.y * 32, 32), :] = mine[:32]
    own_right[1, rows_at(me.y * 32, 32), :] = mine[32:]
    own_part = own_right.at[:, rows_at(me.y * 32, 32)]
    came = [links.to(own_part, own_part, {"dp_0": there}) for there in ys[1:]]
    ortho = three((lh[...], ll[...]), inverse, across)
    ortho_out[...] = ortho
    ob[...] = (ortho * 0.05).astype(BF16)
    for copy in came:
        copy.wait_recv()
    wide[index, :128, :] = own_right[0].astype(BF16)
    wide[index, 128:, :] = own_right[1].astype(BF16)
    gw = HalfGathers(
        me,
        links,
        lambda p: wide.at[index, pl.ds(128 * p, 128)],
        lambda x, c, p: wide.at[2 * x + c, pl.ds(128 * p, 128)],
    )
    values = own_right[...].reshape(256, 256)
    sq[index] = jnp.broadcast_to(jnp.sum(values * values, axis=0, keepdims=True), (8, 256))
    mark = sq.at[index]
    came = [links.to(mark, mark, peer) for peer, _ in me.tensor_peers()]
    gw.first()
    gw.second()
    for copy in came:
        copy.wait_recv()
    squares = sq[0]
    for b in range(1, 8):
        squares += sq[b]
    q_out[...] = values * lax.rsqrt(squares[:1] + 1e-06)
    gw.third()
    gw.rest()
    wide_out[...] = wide[...]
    store.wait()
    links.finish()


def apply_kernel(buf, ob, wide, ortho, q, new_out, ortho_out, q_out):
    for b in range(2):
        cols = slice(256 * b, 256 * b + 256)
        update = lax.dot_general(
            ob[...], wide[b], (((1,), (1,)), ((), ())), preferred_element_type=F32
        )
        new_out[:, cols] = buf[:, cols] - update
    ortho_out[...] = ortho[...]
    q_out[...] = q[...]


def apply_update(buf, ob, wide, ortho, q):
    def rows(height):
        return pl.BlockSpec((height, 256), lambda i: (i, 0))

    cols = pl.BlockSpec((640, 512), lambda i: (0, i))
    return pl.pallas_call(
        apply_kernel,
        grid=(4,),
        out_shape=(
            jax.ShapeDtypeStruct((640, 2048), F32),
            jax.ShapeDtypeStruct((640, 256), F32),
            jax.ShapeDtypeStruct((256, 256), F32),
        ),
        in_specs=[
            cols,
            pl.BlockSpec((640, 256), lambda i: (0, 0)),
            pl.BlockSpec((2, 256, 256), lambda i: (i, 0, 0)),
            rows(160),
            rows(64),
        ],
        out_specs=(cols, rows(160), rows(64)),
        compiler_params=pltpu.CompilerParams(vmem_limit_bytes=24 * 2**20),
        name="apply_update",
    )(buf, ob, wide, ortho, q)


def whole_step(acts, out_grad, momentum, q_basis):
    any_space = pl.BlockSpec(memory_space=pl.ANY)
    in_hbm = pl.BlockSpec(memory_space=pltpu.HBM)
    in_vmem = pl.BlockSpec(memory_space=pltpu.VMEM)
    copies = 140
    vm = pltpu.VMEM
    scratch = [
        vm((1024, 640), BF16),
        vm((4, 640, 256), BF16),
        vm((640, 2048), F32),
        vm((8, 256, 256), F32),
        vm((2048, 256), BF16),
        vm((2048, 256), BF16),
        vm((4, 256, 256), F32),
        vm((4, 256, 256), BF16),
        vm((4, 256, 256), BF16),
        vm((4, 256, 2048), BF16),
        vm((128, 256), F32),
        vm((2, 640, 128), F32),
        vm((2, 3, 160, 128), F32),
        vm((2, 160, 128), F32),
        vm((2, 160, 128), F32),
        vm((7, 40, 128), F32),
        vm((40, 128), F32),
        vm((2, 640, 128), F32),
        vm((2048, 640), BF16),
        vm((2048, 640), BF16),
        vm((640, 256), BF16),
        vm((640, 256), BF16),
        vm((256, 256), F32),
        vm((8, 32, 256), F32),
        vm((32, 256), F32),
        vm((256, 256), F32),
        vm((256, 256), F32),
        vm((4, 2, 256, 256), F32),
        vm((4, 256, 256), F32),
        vm((4, 2, 128, 256), F32),
        vm((3, 128, 256), F32),
        vm((128, 256), F32),
        vm((128, 256), F32),
        vm((3, 4, 32, 256), F32),
        vm((4, 32, 256), F32),
        vm((4, 32, 256), F32),
        vm((3, 32, 256), F32),
        vm((3, 32, 256), F32),
        vm((64, 256), F32),
        vm((7, 8, 256), F32),
        vm((8, 256), F32),
        vm((64, 256), F32),
        vm((2, 128, 256), F32),
        vm((8, 256, 256), BF16),
        vm((8, 8, 256), F32),
        pltpu.SemaphoreType.DMA((copies,)),
        pltpu.SemaphoreType.DMA((copies,)),
        pltpu.SemaphoreType.DMA((12,)),
    ]
    outs = pl.pallas_call(
        step_kernel,
        out_shape=(
            pltpu.VMEM((640, 2048), F32),
            pltpu.VMEM((640, 256), BF16),
            pltpu.VMEM((8, 256, 256), BF16),
            pltpu.VMEM((640, 256), F32),
            pltpu.VMEM((256, 256), F32),
        ),
        in_specs=[in_hbm] * 4,
        out_specs=(in_vmem, in_vmem, in_vmem, in_vmem, in_vmem),
        scratch_shapes=scratch,
        compiler_params=pltpu.CompilerParams(
            collective_id=0, has_side_effects=True, vmem_limit_bytes=56 * 2**20
        ),
        name="whole_step",
    )(acts, out_grad, momentum, q_basis)
    return apply_update(*outs)


def solution(mesh):
    split = Mesh(mesh.devices.reshape(4, 8, 4, 2), ("dp_0", "dp_1", "tensor_0", "tensor_1"))
    return jax.shard_map(
        whole_step,
        mesh=split,
        in_specs=(P(DP, TENSOR), P(DP_TENSOR, None), P(DP_TENSOR, None), P(TENSOR, None)),
        out_specs=(P(DP_TENSOR, None), P(TENSOR, None), P(TENSOR, None)),
        check_vma=False,
    )
```

```python
import jax
import jax.numpy as jnp
from jax import lax
from jax.experimental import pallas as pl
from jax.experimental.pallas import tpu as pltpu
from jax.sharding import Mesh
from jax.sharding import PartitionSpec as P

DP = ("dp_0", "dp_1")
TENSOR = ("tensor_0", "tensor_1")
DP_TENSOR = ("dp_0", "dp_1", "tensor_0", "tensor_1")
HIGH = lax.Precision.HIGHEST
F32, BF16 = jnp.float32, jnp.bfloat16
MESH = pl.DeviceIdType.MESH


def halves(value):
    high = value.astype(BF16)
    return high, (value - high.astype(F32)).astype(BF16)


def mxu(a, b):
    return lax.dot_general(a, b, (((1,), (0,)), ((), ())), preferred_element_type=F32)


class Place:
    def __init__(self):
        self.y, self.z = lax.axis_index("dp_0"), lax.axis_index("dp_1")
        self.x, self.c = lax.axis_index("tensor_0"), lax.axis_index("tensor_1")
        step = 1 - 2 * self.c
        self.sib = 1 - self.c
        self.xp, self.xm = lax.rem(self.x + step + 4, 4), lax.rem(self.x - step + 4, 4)
        self.yp, self.ym = lax.rem(self.y + step + 4, 4), lax.rem(self.y - step + 4, 4)
        self.xo, self.yo = lax.rem(self.x + 2, 4), lax.rem(self.y + 2, 4)

    def tensor_peers(self):
        peers = [({"tensor_1": self.sib}, 2 * self.x + self.sib)]
        for n in range(1, 4):
            there = lax.rem(self.x + n, 4)
            for core in (self.c, self.sib):
                peers.append(({"tensor_0": there, "tensor_1": core}, 2 * there + core))
        return peers

    def zk(self, k):
        return lax.rem(self.z + k, 8)


def greet(me):
    barrier = pltpu.get_barrier_semaphore()
    targets = [peer for peer, _ in me.tensor_peers()]
    targets += [{"dp_0": me.yp}, {"dp_0": me.ym}, {"dp_0": me.yo}]
    targets += [{"dp_1": me.zk(k)} for k in range(1, 8)]
    for target in targets:
        pl.semaphore_signal(barrier, inc=1, device_id=target, device_id_type=MESH)
    pl.semaphore_wait(barrier, len(targets))


class Links:
    def __init__(self, send, recv):
        self.send, self.recv, self.used, self.sent = send, recv, 0, []

    def to(self, src, dst, target):
        copy = pltpu.make_async_remote_copy(
            src_ref=src,
            dst_ref=dst,
            send_sem=self.send.at[self.used],
            recv_sem=self.recv.at[self.used],
            device_id=target,
            device_id_type=MESH,
        )
        self.used += 1
        copy.start()
        self.sent.append(copy)
        return copy

    def finish(self):
        for copy in self.sent:
            copy.wait_send()


class Gather:
    def __init__(self, me, links, own, slot):
        self.me, self.links, self.slot = me, links, slot
        here = slot(me.x, me.c)
        self.a = links.to(own, here, {"tensor_0": me.xp})
        self.b = links.to(own, here, {"tensor_0": me.xm})
        self.s0 = links.to(own, here, {"tensor_1": me.sib})

    def first(self):
        me = self.me
        self.a.wait_recv()
        block = self.slot(me.xm, me.c)
        self.f = self.links.to(block, block, {"tensor_0": me.xp})
        self.s1 = self.links.to(block, block, {"tensor_1": me.sib})

    def second(self):
        me = self.me
        self.b.wait_recv()
        block = self.slot(me.xp, me.c)
        self.s2 = self.links.to(block, block, {"tensor_1": me.sib})

    def third(self):
        me = self.me
        self.f.wait_recv()
        block = self.slot(me.xo, me.c)
        self.s3 = self.links.to(block, block, {"tensor_1": me.sib})

    def rest(self):
        for copy in (self.s0, self.s1, self.s2, self.s3):
            copy.wait_recv()


class RingSum:
    def __init__(self, links, axis, places, src, came, stage):
        own, plus, minus, far = places
        self.links, self.axis, self.src = links, axis, src
        self.own, self.plus, self.came, self.stage = own, plus, came, stage
        self.far = links.to(src(far), came.at[0], {axis: plus})
        self.near = links.to(src(minus), came.at[1], {axis: minus})

    def middle(self):
        self.far.wait_recv()
        self.stage[...] = self.came[0] + self.src(self.plus)[...]
        self.last = self.links.to(self.stage, self.came.at[2], {self.axis: self.plus})

    def total(self):
        self.near.wait_recv()
        self.last.wait_recv()
        return self.src(self.own)[...] + self.came[1] + self.came[2]


class RingSpread:
    def __init__(self, links, axis, places, slot):
        own, plus, minus, _ = places
        self.links, self.axis, self.plus = links, axis, plus
        self.from_minus = slot(minus)
        self.up = links.to(slot(own), slot(own), {axis: plus})
        self.down = links.to(slot(own), slot(own), {axis: minus})

    def middle(self):
        self.up.wait_recv()
        self.far = self.links.to(self.from_minus, self.from_minus, {self.axis: self.plus})

    def finish(self):
        self.down.wait_recv()
        self.far.wait_recv()


class DirectSum:
    def __init__(self, links, axis, places, src, came):
        own, *others = places
        self.mine, self.came = src(own), came
        self.copies = [
            links.to(src(there), came.at[n], {axis: there}) for n, there in enumerate(others)
        ]

    def total(self):
        for copy in self.copies:
            copy.wait_recv()
        return self.mine[...] + self.came[0] + self.came[1] + self.came[2]


class HalfGathers:
    def __init__(self, me, links, own, slot, pieces=2):
        self.parts = [
            Gather(me, links, own(p), lambda x, c, p=p: slot(x, c, p)) for p in range(pieces)
        ]

    def first(self):
        for part in self.parts:
            part.first()

    def second(self):
        for part in self.parts:
            part.second()

    def third(self):
        for part in self.parts:
            part.third()

    def sibling(self, n):
        for part in self.parts:
            getattr(part, "s%d" % n).wait_recv()

    def rest(self):
        for n in range(4):
            self.sibling(n)


def three(a, b, dims=((1,), (0,))):
    dot = lambda p, q: lax.dot_general(p, q, (dims, ((), ())), preferred_element_type=F32)
    return dot(a[0], b[0]) + dot(a[0], b[1]) + dot(a[1], b[0])


def rows_at(start, size, unit=8):
    return pl.ds(pl.multiple_of(start, unit), size)


def eliminate(d):
    lane = lax.broadcasted_iota(jnp.int32, (64, 128), 1)
    row = lax.broadcasted_iota(jnp.int32, (64, 128), 0)
    e = jnp.where(lane < 64, d, jnp.where(lane - 64 == row, 1.0, 0.0).astype(F32))

    def panel(p, e):
        live = 64 - 8 * p
        for first in range(0, 8, 8):
            cols = [jnp.broadcast_to(e[:, j : j + 1], (64, 128)) for j in range(first, first + 8)]
            for n, col in enumerate(cols):
                j = first + n
                weight = pltpu.reciprocal(col[j : j + 1])
                factor = jnp.where((row > j) & (row < live), col, 0.0) * weight
                e = e - factor * e[j : j + 1]
                for m in range(n + 1, 8):
                    cols[m] = cols[m] - factor * col[first + m : first + m + 1]
        e = pltpu.roll(e, 120, 1)
        return jnp.concatenate([e[8:], e[:8]], axis=0)

    e = lax.fori_loop(0, 8, panel, e)
    v = e[:, :64]
    diag = jnp.sum(jnp.where(lane - 64 == row, e, 0.0), axis=1, keepdims=True)
    return v * lax.rsqrt(diag)


def exact(a, b, dims=((1,), (0,))):
    return lax.dot_general(a, b, (dims, ((), ())), precision=HIGH, preferred_element_type=F32)


def factor_block(k, a, inv):
    rows = slice(64 * k, 64 * k + 64)
    block = a[rows, 128 * (k // 2) : 128 * (k // 2) + 128]
    if k % 2:
        block = pltpu.roll(block, 64, 1)
    v = eliminate(block)
    inv_row = exact(v, inv[rows, :])
    inv[rows, :] = inv_row
    if k < 3:
        u = exact(v, a[rows, :])
        below = u.T[64 * (k + 1) :, :]
        rest = slice(64 * (k + 1), 256)
        a[rest, :] = a[rest, :] - exact(below, u)
        inv[rest, :] = inv[rest, :] - exact(below, inv_row)


def step_kernel(
    acts, og, mom, q, buf_out, ob, wide_out, ortho_out, q_out,
    actsv, acts_t, buf, qg, qh, ql, yg, yh, yl, ogg, y_own,
    part, r_left, s1, chunk, zr, zs, full,
    bth, btl, lh, ll, gram, gram_r, gram_s, a, inv,
    cc, c_sib, c_sum, rx, sx, tx, ry, sy, ty, rxy, ryx,
    rest, zr2, zs2, all_z, own_right, wide, sq,
    send, recv, local,
):
    me = Place()
    links = Links(send, recv)
    own_q = qg.at[me.x * 2 + me.c]
    own_rows = pl.ds(pl.multiple_of(me.c * 128, 128), 128)
    own_og = ogg.at[me.x, own_rows]
    loads = [
        pltpu.make_async_copy(q, own_q, local.at[0]),
        pltpu.make_async_copy(og, own_og, local.at[1]),
        pltpu.make_async_copy(acts, actsv, local.at[2]),
        pltpu.make_async_copy(mom, buf, local.at[3]),
    ]
    for load in loads:
        load.start()
    greet(me)
    gq = HalfGathers(
        me,
        links,
        lambda p: q.at[pl.ds(64 * p, 64)],
        lambda x, c, p: qg.at[x * 2 + c, pl.ds(64 * p, 64)],
        pieces=4,
    )
    gq.first()
    gq.second()
    loads[2].wait()
    for j in range(4):
        acts_t[j] = actsv[256 * j : 256 * (j + 1), :].T
    loads[0].wait()
    loads[1].wait()
    loads[3].wait()
    own = ogg.at[me.x, own_rows]

    def take(x, c, first=False):
        b = 2 * x + c
        rows = rows_at(b * 256, 256, 256)
        high, low = halves(qg[b])
        qh[rows, :], ql[rows, :] = high, low
        lhs = own[:, rows]
        share = mxu(lhs, high) + mxu(lhs, low)
        y_own[...] = share if first else y_own[...] + share

    take(me.x, me.c, True)
    take(me.xm, me.c)
    take(me.xp, me.c)
    gq.sibling(0)
    take(me.x, me.sib)
    gq.third()
    take(me.xo, me.c)
    gq.sibling(1)
    take(me.xp, me.sib)
    gq.sibling(2)
    take(me.xm, me.sib)
    gq.sibling(3)
    take(me.xo, me.sib)
    yg[me.x, own_rows, :] = y_own[...]
    def y_piece(x, c, p):
        return yg.at[x, rows_at(c * 128 + 64 * p, 64, 64)]

    gy = HalfGathers(me, links, lambda p: y_piece(me.x, me.c, p), y_piece)

    def momentum_part(t):
        rows = rows_at(t * 128, 128)
        share = three(halves(buf[rows, :]), (qh[...], ql[...]))
        for half in range(2):
            part[half, rows, :] = share[:, 128 * half : 128 * half + 128]

    pl.loop(0, 3)(momentum_part)
    gy.first()
    gy.second()
    pl.loop(3, 5)(momentum_part)
    gy.third()
    gy.rest()
    go = Gather(
        me, links, og, lambda x, c: ogg.at[x, pl.ds(pl.multiple_of(c * 128, 128), 128)]
    )
    for j in range(4):
        high, low = halves(yg[j])
        yh[j], yl[j] = high, low

    @pl.loop(0, 5)
    def _(t):
        rows = pl.ds(pl.multiple_of(t * 128, 128), 128)
        acc = jnp.zeros((128, 256), F32)
        for j in range(4):
            lhs = acts_t[j, rows, :]
            acc += mxu(lhs, yh[j]) + mxu(lhs, yl[j])
        for half in range(2):
            piece = acc[:, 128 * half : 128 * half + 128]
            part[half, rows, :] = (0.95 * part[half, rows, :] + piece) * (1 / 32)

    ys, xs = (me.y, me.yp, me.ym, me.yo), (me.x, me.xp, me.xm, me.xo)
    rings = [
        RingSum(
            links,
            "dp_0",
            ys,
            lambda y, h=h: part.at[h, rows_at(y * 160, 160, 32)],
            r_left.at[h],
            s1.at[h],
        )
        for h in range(2)
    ]
    for ring in rings:
        ring.middle()
    for h in range(2):
        chunk[h] = rings[h].total()

    def z_rows(z):
        return z // 4, pl.multiple_of(lax.rem(z, 4) * 40, 8)

    came = []
    for k in range(1, 8):
        half, row = z_rows(me.zk(k))
        came.append(
            links.to(chunk.at[half, pl.ds(row, 40)], zr.at[k - 1], {"dp_1": me.zk(k)})
        )
    go.first()
    go.second()
    half, row = z_rows(me.z)
    for copy in came:
        copy.wait_recv()
    total = chunk[half, pl.ds(row, 40), :]
    for k in range(7):
        total += zr[k]
    zs[...] = total
    spot = full.at[half, pl.ds(pl.multiple_of(me.y * 160 + row, 8), 40)]
    came = [links.to(zs, spot, {"dp_1": me.zk(k)}) for k in range(1, 8)]
    spot[...] = total
    go.third()
    for copy in came:
        copy.wait_recv()
    spreads = [
        RingSpread(links, "dp_0", ys, lambda y, h=h: full.at[h, rows_at(y * 160, 160, 32)])
        for h in range(2)
    ]

    def buffer_part(n):
        cols = rows_at(n * 256, 256, 256)
        acc = 0.95 * buf[:, cols]
        for j in range(4):
            acc += mxu(acts_t[j], ogg[j, :, cols])
        buf[:, cols] = acc
        bth[cols, :], btl[cols, :] = halves(acc.T)

    go.rest()
    pl.loop(0, 4)(buffer_part)
    for spread in spreads:
        spread.middle()
    pl.loop(4, 8)(buffer_part)
    store = pltpu.make_async_copy(buf, buf_out, local.at[4])
    store.start()
    for spread in spreads:
        spread.finish()
    lt = []
    for half in range(2):
        cols = slice(128 * half, 128 * half + 128)
        lh[:, cols], ll[:, cols] = halves(full[half])
        lt.append(full[half].T)
    left = lh[...], ll[...]
    gram[...] = three(halves(jnp.concatenate(lt, axis=0)), left)

    def product_with(core):
        @pl.loop(0, 4)
        def _(n):
            rows = rows_at((2 * n + core) * 256, 256, 256)
            cc[n, core] = three((bth[rows, :], btl[rows, :]), (lh[...], ll[...]))

    index = 2 * me.x + me.c
    gram_in = []
    for peer, there in me.tensor_peers():
        gram_in.append(links.to(gram.at[rows_at(there * 32, 32)], gram_r.at[index], peer))
    gram_r[index] = gram[rows_at(index * 32, 32), :]
    product_with(me.sib)
    swap = links.to(cc.at[:, me.sib], c_sib, {"tensor_1": me.sib})
    for copy in gram_in:
        copy.wait_recv()
    total = gram_r[0]
    for b in range(1, 8):
        total += gram_r[b]
    gram_s[...] = total
    gram_rows = a.at[rows_at(index * 32, 32)]
    gram_in = [links.to(gram_s, gram_rows, peer) for peer, _ in me.tensor_peers()]
    gram_rows[...] = total
    product_with(me.c)
    swap.wait_recv()
    c_sum[...] = cc[:, me.c].reshape(4, 2, 128, 256) + c_sib[...].reshape(4, 2, 128, 256)
    x_first = RingSum(links, "tensor_0", xs, lambda x: c_sum.at[x, 0], rx, sx)
    y_first = RingSum(
        links, "dp_0", ys, lambda y: c_sum.at[:, 1, rows_at(y * 32, 32)], ry, sy
    )
    same = lax.broadcasted_iota(jnp.int32, (256, 256), 0) == lax.broadcasted_iota(
        jnp.int32, (256, 256), 1
    )
    inv[...] = jnp.where(same, 1.0, 0.0).astype(F32)
    for copy in gram_in:
        copy.wait_recv()
    factor_block(0, a, inv)
    y_first.middle()
    x_first.middle()
    factor_block(1, a, inv)
    tx[...] = x_first.total()
    then_y = DirectSum(links, "dp_0", ys, lambda y: tx.at[rows_at(y * 32, 32)], ryx)
    ty[...] = y_first.total()
    then_x = DirectSum(links, "tensor_0", xs, lambda x: ty.at[x], rxy)
    factor_block(2, a, inv)
    rest[:32, :] = then_y.total()
    rest[32:, :] = then_x.total()
    came = [
        links.to(rest.at[rows_at(me.zk(k) * 8, 8)], zr2.at[k - 1], {"dp_1": me.zk(k)})
        for k in range(1, 8)
    ]
    factor_block(3, a, inv)
    for copy in came:
        copy.wait_recv()
    total = rest[rows_at(me.z * 8, 8), :]
    for k in range(7):
        total += zr2[k]
    total = total * (1 / 32)
    zs2[...] = total
    spot = all_z.at[rows_at(me.z * 8, 8)]
    came = [links.to(zs2, spot, {"dp_1": me.zk(k)}) for k in range(1, 8)]
    spot[...] = total
    inverse = halves(inv[...])
    across = ((1,), (1,))
    for copy in came:
        copy.wait_recv()
    mine = three(halves(all_z[...]), inverse, across)
    own_right[0, rows_at(me.y * 32, 32), :] = mine[:32]
    own_right[1, rows_at(me.y * 32, 32), :] = mine[32:]
    own_part = own_right.at[:, rows_at(me.y * 32, 32)]
    came = [links.to(own_part, own_part, {"dp_0": there}) for there in ys[1:]]
    ortho = three((lh[...], ll[...]), inverse, across)
    ortho_out[...] = ortho
    ob[...] = (ortho * 0.05).astype(BF16)
    for copy in came:
        copy.wait_recv()
    wide[index, :128, :] = own_right[0].astype(BF16)
    wide[index, 128:, :] = own_right[1].astype(BF16)
    gw = HalfGathers(
        me,
        links,
        lambda p: wide.at[index, pl.ds(128 * p, 128)],
        lambda x, c, p: wide.at[2 * x + c, pl.ds(128 * p, 128)],
    )
    values = own_right[...].reshape(256, 256)
    sq[index] = jnp.broadcast_to(jnp.sum(values * values, axis=0, keepdims=True), (8, 256))
    mark = sq.at[index]
    came = [links.to(mark, mark, peer) for peer, _ in me.tensor_peers()]
    gw.first()
    gw.second()
    for copy in came:
        copy.wait_recv()
    squares = sq[0]
    for b in range(1, 8):
        squares += sq[b]
    q_out[...] = values * lax.rsqrt(squares[:1] + 1e-06)
    gw.third()
    gw.rest()
    wide_out[...] = wide[...]
    store.wait()
    links.finish()


def apply_kernel(buf, ob, wide, ortho, q, new_out, ortho_out, q_out):
    for b in range(2):
        cols = slice(256 * b, 256 * b + 256)
        update = lax.dot_general(
            ob[...], wide[b], (((1,), (1,)), ((), ())), preferred_element_type=F32
        )
        new_out[:, cols] = buf[:, cols] - update
    ortho_out[...] = ortho[...]
    q_out[...] = q[...]


def apply_update(buf, ob, wide, ortho, q):
    def rows(height):
        return pl.BlockSpec((height, 256), lambda i: (i, 0))

    cols = pl.BlockSpec((640, 512), lambda i: (0, i))
    return pl.pallas_call(
        apply_kernel,
        grid=(4,),
        out_shape=(
            jax.ShapeDtypeStruct((640, 2048), F32),
            jax.ShapeDtypeStruct((640, 256), F32),
            jax.ShapeDtypeStruct((256, 256), F32),
        ),
        in_specs=[
            cols,
            pl.BlockSpec((640, 256), lambda i: (0, 0)),
            pl.BlockSpec((2, 256, 256), lambda i: (i, 0, 0)),
            rows(160),
            rows(64),
        ],
        out_specs=(cols, rows(160), rows(64)),
        compiler_params=pltpu.CompilerParams(vmem_limit_bytes=24 * 2**20),
        name="apply_update",
    )(buf, ob, wide, ortho, q)


def whole_step(acts, out_grad, momentum, q_basis):
    any_space = pl.BlockSpec(memory_space=pl.ANY)
    in_hbm = pl.BlockSpec(memory_space=pltpu.HBM)
    in_vmem = pl.BlockSpec(memory_space=pltpu.VMEM)
    copies = 160
    vm = pltpu.VMEM
    scratch = [
        vm((1024, 640), BF16),
        vm((4, 640, 256), BF16),
        vm((640, 2048), F32),
        vm((8, 256, 256), F32),
        vm((2048, 256), BF16),
        vm((2048, 256), BF16),
        vm((4, 256, 256), F32),
        vm((4, 256, 256), BF16),
        vm((4, 256, 256), BF16),
        vm((4, 256, 2048), BF16),
        vm((128, 256), F32),
        vm((2, 640, 128), F32),
        vm((2, 3, 160, 128), F32),
        vm((2, 160, 128), F32),
        vm((2, 160, 128), F32),
        vm((7, 40, 128), F32),
        vm((40, 128), F32),
        vm((2, 640, 128), F32),
        vm((2048, 640), BF16),
        vm((2048, 640), BF16),
        vm((640, 256), BF16),
        vm((640, 256), BF16),
        vm((256, 256), F32),
        vm((8, 32, 256), F32),
        vm((32, 256), F32),
        vm((256, 256), F32),
        vm((256, 256), F32),
        vm((4, 2, 256, 256), F32),
        vm((4, 256, 256), F32),
        vm((4, 2, 128, 256), F32),
        vm((3, 128, 256), F32),
        vm((128, 256), F32),
        vm((128, 256), F32),
        vm((3, 4, 32, 256), F32),
        vm((4, 32, 256), F32),
        vm((4, 32, 256), F32),
        vm((3, 32, 256), F32),
        vm((3, 32, 256), F32),
        vm((64, 256), F32),
        vm((7, 8, 256), F32),
        vm((8, 256), F32),
        vm((64, 256), F32),
        vm((2, 128, 256), F32),
        vm((8, 256, 256), BF16),
        vm((8, 8, 256), F32),
        pltpu.SemaphoreType.DMA((copies,)),
        pltpu.SemaphoreType.DMA((copies,)),
        pltpu.SemaphoreType.DMA((12,)),
    ]
    outs = pl.pallas_call(
        step_kernel,
        out_shape=(
            pltpu.VMEM((640, 2048), F32),
            pltpu.VMEM((640, 256), BF16),
            pltpu.VMEM((8, 256, 256), BF16),
            pltpu.VMEM((640, 256), F32),
            pltpu.VMEM((256, 256), F32),
        ),
        in_specs=[in_hbm] * 4,
        out_specs=(in_vmem, in_vmem, in_vmem, in_vmem, in_vmem),
        scratch_shapes=scratch,
        compiler_params=pltpu.CompilerParams(
            collective_id=0, has_side_effects=True, vmem_limit_bytes=56 * 2**20
        ),
        name="whole_step",
    )(acts, out_grad, momentum, q_basis)
    return apply_update(*outs)


def solution(mesh):
    split = Mesh(mesh.devices.reshape(4, 8, 4, 2), ("dp_0", "dp_1", "tensor_0", "tensor_1"))
    return jax.shard_map(
        whole_step,
        mesh=split,
        in_specs=(P(DP, TENSOR), P(DP_TENSOR, None), P(DP_TENSOR, None), P(TENSOR, None)),
        out_specs=(P(DP_TENSOR, None), P(TENSOR, None), P(TENSOR, None)),
        check_vma=False,
    )
```
